32 devices in a mesh: traj: 8 (over z, y), seg: 4 (over x, core).
Axes of the slice: x: 2, y: 2, z: 4, core: 2. Of those that a mesh axis runs over, the one named last changes fastest.
Arguments:
- coords: float32 [8, 512, 3, 512], P('traj', 'seg')
- pairs: int32 [2, 1024], replicated, may hold values from 0 to 511, as said below
- lengths: int32 [8], P('traj'), may hold values from 1 to 512, 3072 in all
Outputs:
- projected: float32 [8, 512, 128], P('traj', 'seg')
The draws below stay inside these ranges and needn't reach their ends.
Inputs may be any that keep to these rules, and one draw needn't show every extreme that they name: `pairs`: atom indices; the two atoms of a contact differ. `lengths`: each trajectory's recorded frames fill its first slots.
All inputs are finite; a program needn't handle non-finite values. No bound on the sum of `lengths` on one device may be relied on, other than what follows from the above.
Results may differ from the reference program's by a relative error of at most 0.0003.
Values sent between devices are 32-bit elements; how exact they have to be, the bound alone decides.
A program may use at most 128 MiB of HBM per device.

```python
import math
import jax
import jax.numpy as jnp
import numpy as np
from jax import lax

FEAT = 1024
K = 128
ATOMS = 512
LAG = 10
ITERS = 3
TRAJS = 8
SEG_LEN = 512


def draw_coords(key, part):
    keys = jax.random.split(jax.random.fold_in(key, 7), 6)
    shared_base = jax.random.normal(keys[0], (1, 1, 3, ATOMS), jnp.float32) * 1.5
    own_base = jax.random.normal(keys[1], (TRAJS, 1, 3, ATOMS), jnp.float32) * 0.3
    amplitude = jax.random.uniform(keys[2], (TRAJS, 1, 3, ATOMS), jnp.float32, 0.2, 0.8)
    log_freq = jax.random.uniform(keys[3], (1, 1, 1, ATOMS), jnp.float32, math.log(0.005), math.log(0.1))
    phase = jax.random.uniform(keys[4], (TRAJS, 1, 3, ATOMS), jnp.float32, -math.pi, math.pi)
    times = jnp.arange(SEG_LEN, dtype=jnp.float32).reshape(1, SEG_LEN, 1, 1)
    shape = (TRAJS, SEG_LEN, 3, ATOMS)
    noise = jax.random.normal(keys[5], shape, jnp.float32) * 0.3
    motion = amplitude * jnp.sin(jnp.exp(log_freq) * times + phase)
    return shared_base + own_base + motion + noise


def draw_pairs(key, part):
    keys = jax.random.split(jax.random.fold_in(key, 11), 2)
    first_atom = jax.random.randint(keys[0], (FEAT,), 0, ATOMS, jnp.int32)
    offset = jax.random.randint(keys[1], (FEAT,), 1, ATOMS, jnp.int32)
    second_atom = (first_atom + offset) % ATOMS
    first_atom = first_atom.at[0].set(0)
    second_atom = second_atom.at[0].set(ATOMS - 1)
    return jnp.stack([first_atom, second_atom]).astype(jnp.int32)


def profile(number_of, total, reach, slope):
    loads = [(1 << 20) // math.isqrt(standing ** slope) + 1 for standing in range(2, number_of + 1)]
    spare, given = total - reach - (number_of - 1), [1] * (number_of - 1)
    while spare > 0:
        movable = [i for i in range(number_of - 1) if given[i] < reach]
        whole, left = sum([loads[i] for i in movable]), spare
        for i in movable:
            more = min(reach - given[i], max(1, left * loads[i] // whole), spare)
            given[i] = given[i] + more
            spare = spare - more
    return np.array([reach] + given)


def uneven(key, amount, total, limit, skew):
    if amount == 2:
        one = jax.random.randint(key, (), max(1, total - limit), min(limit, total - 1) + 1)
        return jnp.stack([one, total - one])
    tallies = jnp.asarray(profile(amount, total, limit, skew), jnp.int32)
    couples = (amount - 1) // 2
    source_of, sink = tallies[1:1 + 2 * couples:2], tallies[2:2 + 2 * couples:2]
    slack = jnp.minimum(source_of - 1, limit - sink)
    passed = jax.random.randint(jax.random.fold_in(key, 1), (couples,), 0, 1 << 20) % (slack + 1)
    tallies = tallies.at[1:1 + 2 * couples:2].set(source_of - passed).at[2:2 + 2 * couples:2].set(sink + passed)
    return tallies[jax.random.permutation(jax.random.fold_in(key, 2), amount)]


def setup_inputs(seed: int = 0) -> dict:
    splits = jax.random.split(jax.random.key(seed), 4)
    return {
        "coords": draw_coords(jax.random.fold_in(splits[3], 71), 0),
        "pairs": draw_pairs(jax.random.fold_in(splits[3], 71), 0),
        "lengths": uneven(splits[2], TRAJS, TRAJS * SEG_LEN * 3 // 4, SEG_LEN, 1).astype(jnp.int32),
    }


exact_mode = lax.Precision.HIGHEST
soft_square = 0.1
ridge_term = 0.01
spectral_shift = 2.0

def featurize(frames, pairs):
    first_atom = jnp.take(frames, pairs[0], axis=2)
    second_atom = jnp.take(frames, pairs[1], axis=2)
    offset = first_atom - second_atom
    return jnp.sqrt(lax.optimization_barrier(jnp.sum(offset * offset, axis=1)) + soft_square)

def tri_solve(factor, rhs, transposed):
    return lax.linalg.triangular_solve(factor, rhs, left_side=True, lower=True, transpose_a=transposed)

def cross_gram(left_rows, right_rows):
    return lax.dot_general(left_rows.astype(jnp.float32), right_rows.astype(jnp.float32), (((0,), (0,)), ((), ())), precision=exact_mode, preferred_element_type=jnp.float32)

def subspace(c_zero, c_lag, basis_width):
    lower_factor = jnp.linalg.cholesky(c_zero)
    identity = jnp.eye(c_zero.shape[0], dtype=jnp.float32)
    basis_q = identity[:, :basis_width]
    for sweep in range(ITERS):
        inner_solve = tri_solve(lower_factor, basis_q, True)
        moved_block = jnp.dot(c_lag.astype(jnp.float32), inner_solve.astype(jnp.float32), precision=exact_mode, preferred_element_type=jnp.float32)
        image_block = tri_solve(lower_factor, moved_block, False) + spectral_shift * basis_q
        gram_small = cross_gram(image_block, image_block)
        small_factor = jnp.linalg.cholesky(gram_small)
        basis_q = tri_solve(small_factor, image_block.T, False).T
    return tri_solve(lower_factor, basis_q, True)

def reference(coords, pairs, lengths):
    frame_index = jnp.arange(SEG_LEN, dtype=jnp.int32)
    feature_count = pairs.shape[1]

    def masks_of(length):
        is_valid = (frame_index < length).astype(jnp.float32)
        paired = (frame_index + LAG < length).astype(jnp.float32)
        return (is_valid, paired)

    def lagged_of(features):
        return jnp.concatenate([features[LAG:], jnp.zeros((LAG, feature_count), jnp.float32)], axis=0)

    def first_pass(running, inputs):
        frames, length = inputs
        features = featurize(frames, pairs)
        is_valid, paired = masks_of(length)
        lagged = lagged_of(features)
        updated = (running[0] + jnp.sum(is_valid), running[1] + jnp.sum(paired), running[2] + jnp.dot(is_valid.astype(jnp.float32), features.astype(jnp.float32), precision=exact_mode, preferred_element_type=jnp.float32), running[3] + jnp.dot(paired.astype(jnp.float32), features.astype(jnp.float32), precision=exact_mode, preferred_element_type=jnp.float32), running[4] + jnp.dot(paired.astype(jnp.float32), lagged.astype(jnp.float32), precision=exact_mode, preferred_element_type=jnp.float32))
        return (updated, None)
    zero_scalar = jnp.zeros((), jnp.float32)
    zero_vector = jnp.zeros((feature_count,), jnp.float32)
    sums_out, unused = lax.scan(first_pass, (zero_scalar, zero_scalar, zero_vector, zero_vector, zero_vector), (coords, lengths))
    frames_total, pairs_total = (sums_out[0], sums_out[1])
    mean_all = sums_out[2] / frames_total
    mean_lead = sums_out[3] / pairs_total
    mean_ahead = sums_out[4] / pairs_total

    def second_pass(running, inputs):
        frames, length = inputs
        features = featurize(frames, pairs)
        is_valid, paired = masks_of(length)
        lagged = lagged_of(features)
        centered = (features - mean_all) * is_valid[:, None]
        lead_rows = (features - mean_lead) * paired[:, None]
        ahead_rows = (lagged - mean_ahead) * paired[:, None]
        return ((running[0] + cross_gram(centered, centered), running[1] + cross_gram(lead_rows, ahead_rows)), None)
    zero_matrix = jnp.zeros((feature_count, feature_count), jnp.float32)
    grams, unused = lax.scan(second_pass, (zero_matrix, zero_matrix), (coords, lengths))
    identity = jnp.eye(feature_count, dtype=jnp.float32)
    c_zero = grams[0] / frames_total + ridge_term * identity
    c_lag = (grams[1] + grams[1].T) / (2.0 * pairs_total)
    basis = subspace(c_zero, c_lag, K)

    def project(inputs):
        frames, length = inputs
        features = featurize(frames, pairs)
        is_valid, paired = masks_of(length)
        centered = (features - mean_all) * is_valid[:, None]
        return jnp.dot(centered.astype(jnp.float32), basis.astype(jnp.float32), precision=exact_mode, preferred_element_type=jnp.float32)
    return lax.map(project, (coords, lengths))
```

```python
import jax
import jax.numpy as jnp
from jax import lax
from jax.experimental import pallas as pl
from jax.experimental.pallas import tpu as pltpu
from jax.sharding import PartitionSpec as P

K = 128
LAG = 10
ITERS = 3
BLOCK = 128
GROUP = 4


exact_mode = lax.Precision.HIGHEST
soft_square = 0.1
ridge_term = 0.01
spectral_shift = 2.0


def exact_dot(left, right, left_axis=1, right_axis=0):
    return lax.dot_general(
        left,
        right,
        (((left_axis,), (right_axis,)), ((), ())),
        precision=exact_mode,
        preferred_element_type=jnp.float32,
    )


def split3(x):
    high = x.astype(jnp.bfloat16)
    rest = x - high.astype(jnp.float32)
    middle = rest.astype(jnp.bfloat16)
    low = (rest - middle.astype(jnp.float32)).astype(jnp.bfloat16)
    return high, middle, low


def inverse_factor(matrix):
    size = matrix.shape[0]
    lane = lax.broadcasted_iota(jnp.int32, (8, size), 1)
    sub = lax.broadcasted_iota(jnp.int32, (8, size), 0)
    rest = matrix.reshape(size // 8, 8, size)
    finished = []
    for start in range(0, size, GROUP):
        top = start % 8
        head = rest[0]
        pivots = [
            [
                jnp.broadcast_to(head[top + a : top + a + 1, start + b : start + b + 1], (8, size))
                if b >= a
                else None
                for b in range(GROUP)
            ]
            for a in range(GROUP)
        ]
        columns = [
            jnp.broadcast_to(rest[:, :, start + a : start + a + 1], rest.shape)
            for a in range(GROUP)
        ]
        rows, inverses = [], []
        for a in range(GROUP):
            row = jnp.broadcast_to(head[top + a : top + a + 1, :], (8, size))
            row = jnp.where((lane >= start) & (lane < start + GROUP), 0.0, row)
            for b in range(a):
                row = row - (pivots[b][a] * inverses[b]) * rows[b]
            inverse = 1.0 / pivots[a][a]
            for b in range(a + 1, GROUP):
                scale = pivots[a][b] * inverse
                for c in range(b, GROUP):
                    pivots[b][c] = pivots[b][c] - scale * pivots[a][c]
            rows.append(jnp.where(lane == start + a, 1.0, row))
            inverses.append(inverse)
        scaled = []
        for a in range(GROUP):
            column = columns[a]
            for b in range(a):
                column = column - scaled[b] * pivots[b][a][None]
            scaled.append(column * inverses[a][None])
        cleared = jnp.where(((lane >= start) & (lane < start + GROUP))[None], 0.0, rest)
        update = scaled[0] * rows[0][None]
        for a in range(1, GROUP):
            update = update + scaled[a] * rows[a][None]
        fresh = cleared - update
        head = jnp.where(sub >= top + GROUP, fresh[0], head)
        for a in range(GROUP):
            head = jnp.where(sub == top + a, rows[a] * jnp.sqrt(inverses[a]), head)
        if top + GROUP == 8:
            finished.append(head)
            rest = fresh[1:] if start + GROUP < size else None
        else:
            rest = jnp.concatenate([head[None], fresh[1:]], axis=0) if len(fresh) > 1 else head[None]
    out = jnp.concatenate(finished, axis=0)
    row_index = lax.broadcasted_iota(jnp.int32, (size, size), 0)
    lane_index = lax.broadcasted_iota(jnp.int32, (size, size), 1)
    return jnp.where(lane_index <= row_index, out, 0.0)


def small_factor_kernel(gram_ref, out_ref):
    out_ref[...] = inverse_factor(gram_ref[...])


def small_factor(gram):
    return pl.pallas_call(
        small_factor_kernel,
        out_shape=jax.ShapeDtypeStruct(gram.shape, jnp.float32),
        name="small_factor",
    )(gram)


def inverse_kernel(tile, matrix_ref, out_ref, first_ref, wide):
    size = matrix_ref.shape[0]

    @pl.loop(0, size // tile)
    def _(i):
        span = pl.ds(pl.multiple_of(i * tile, tile), tile)
        out_ref[span, :] = matrix_ref[span, :]

    @pl.loop(0, size // BLOCK)
    def _(k):
        here = pl.ds(pl.multiple_of(k * BLOCK, BLOCK), BLOCK)
        factor = inverse_factor(out_ref[here, here])

        @pl.when(k == 0)
        def _():
            first_ref[...] = factor

        pivot = exact_dot(factor, factor, 0, 0)
        row = exact_dot(pivot, out_ref[here, :])
        high, middle, low = split3(row)
        for place, piece in enumerate((high, middle, high, middle, low, high)):
            wide[place * BLOCK : (place + 1) * BLOCK, :] = piece

        @pl.loop(0, size // tile)
        def _(i):
            span = pl.ds(pl.multiple_of(i * tile, tile), tile)
            column = out_ref[span, here]
            h, m, l = split3(column)
            long = jnp.concatenate([h, h, m, m, h, l], axis=1)
            out_ref[span, :] -= jnp.dot(long, wide[...], preferred_element_type=jnp.float32)
            out_ref[span, here] = exact_dot(column, pivot)

        out_ref[here, :] = row
        out_ref[here, here] = -pivot


def negative_inverse(matrix):
    size = matrix.shape[0]
    tile = min(256, size)
    return pl.pallas_call(
        lambda *refs: inverse_kernel(tile, *refs),
        out_shape=(
            jax.ShapeDtypeStruct((size, size), jnp.float32),
            jax.ShapeDtypeStruct((BLOCK, BLOCK), jnp.float32),
        ),
        in_specs=[pl.BlockSpec(memory_space=pltpu.VMEM)],
        out_specs=(
            pl.BlockSpec(memory_space=pltpu.VMEM),
            pl.BlockSpec(memory_space=pltpu.VMEM),
        ),
        scratch_shapes=[pltpu.VMEM((6 * BLOCK, size), jnp.bfloat16)],
        compiler_params=pltpu.CompilerParams(vmem_limit_bytes=40 * 1024 * 1024),
        cost_estimate=pl.CostEstimate(
            flops=120 * size * size * size, bytes_accessed=8 * size * size, transcendentals=0
        ),
        name="negative_inverse",
    )(matrix)


def featurize(frames, selection):
    frame_rows, parts, atoms = frames.shape
    offset = exact_dot(jnp.swapaxes(frames, 0, 1).reshape(parts * frame_rows, atoms), selection)
    offset = offset.reshape(parts, frame_rows, -1)
    return jnp.sqrt(jnp.sum(offset * offset, axis=0) + soft_square)


def on_device(coords, pairs, lengths):
    frames = coords[0]
    frame_rows, _, atoms = frames.shape
    feature_count = pairs.shape[1]
    trajs, segs = lax.axis_size("traj"), lax.axis_size("seg")
    devices = trajs * segs
    traj, seg = lax.axis_index("traj"), lax.axis_index("seg")
    me = traj * segs + seg
    length = lengths[0]

    arriving = lax.ppermute(frames[:LAG], "seg", [(i + 1, i) for i in range(segs - 1)])
    atom = jnp.arange(atoms, dtype=jnp.int32)[:, None]
    selection = (atom == pairs[0][None]).astype(jnp.float32) - (atom == pairs[1][None]).astype(
        jnp.float32
    )
    features = featurize(frames, selection)
    lagged = jnp.concatenate([features[LAG:], featurize(arriving, selection)], axis=0)

    frame_index = seg * frame_rows + jnp.arange(frame_rows, dtype=jnp.int32)
    is_valid = (frame_index < length).astype(jnp.float32)[:, None]
    paired = (frame_index + LAG < length).astype(jnp.float32)[:, None]
    count_all = jnp.maximum(jnp.sum(is_valid), 1.0)
    count_pair = jnp.maximum(jnp.sum(paired), 1.0)
    own_all = jnp.sum(features * is_valid, axis=0) / count_all
    own_lead = jnp.sum(features * paired, axis=0) / count_pair
    own_ahead = jnp.sum(lagged * paired, axis=0) / count_pair
    centered = (features - own_all) * is_valid
    lead_rows = (features - own_lead) * paired
    ahead_rows = (lagged - own_ahead) * paired
    gram_zero = exact_dot(centered, centered, 0, 0)
    gram_lag = exact_dot(
        jnp.concatenate([lead_rows, ahead_rows], axis=0),
        jnp.concatenate([ahead_rows, lead_rows], axis=0),
        0,
        0,
    )

    mine = (jnp.arange(devices) == me)[:, None]
    slot_all = jnp.where(mine, own_all[None], 0.0)
    slot_lag = jnp.concatenate(
        [jnp.where(mine, own_lead[None], 0.0), jnp.where(mine, own_ahead[None], 0.0)], axis=0
    )
    slot_length = jnp.where(
        (jnp.arange(trajs) == traj) & (seg == 0), length.astype(jnp.float32), 0.0
    )
    slot_length = jnp.pad(slot_length[None], ((0, 7), (0, feature_count - trajs)))
    first_load = jnp.concatenate([gram_zero, slot_all, slot_length], axis=0)
    first_total = lax.psum(first_load, ("traj", "seg"))
    second_load = jnp.concatenate([gram_lag, slot_lag], axis=0)
    second_load, first_total = lax.optimization_barrier((second_load, first_total))
    second_total = lax.psum(second_load, ("traj", "seg"))

    all_lengths = first_total[feature_count + devices, :trajs]
    begins = jnp.arange(segs, dtype=jnp.float32)[None] * frame_rows
    counts = jnp.clip(all_lengths[:, None] - begins, 0.0, frame_rows).reshape(devices, 1)
    pair_counts = jnp.clip(all_lengths[:, None] - LAG - begins, 0.0, frame_rows).reshape(devices, 1)
    frames_total, pairs_total = jnp.sum(counts), jnp.sum(pair_counts)
    device_all = first_total[feature_count : feature_count + devices]
    mean_all = jnp.sum(device_all * counts, axis=0) / frames_total
    spread_all = device_all - mean_all
    total_zero = first_total[:feature_count] + exact_dot(spread_all * counts, spread_all, 0, 0)
    c_zero = total_zero / frames_total + ridge_term * jnp.eye(feature_count, dtype=jnp.float32)
    inverse, first_factor = negative_inverse(c_zero)

    device_lead = second_total[feature_count : feature_count + devices]
    device_ahead = second_total[feature_count + devices :]
    spread_lead = device_lead - jnp.sum(device_lead * pair_counts, axis=0) / pairs_total
    spread_ahead = device_ahead - jnp.sum(device_ahead * pair_counts, axis=0) / pairs_total
    between = exact_dot(
        jnp.concatenate([spread_lead * pair_counts, spread_ahead * pair_counts], axis=0),
        jnp.concatenate([spread_ahead, spread_lead], axis=0),
        0,
        0,
    )
    c_lag = (second_total[:feature_count] + between) / (2.0 * pairs_total)

    seed = exact_dot(jnp.eye(BLOCK, dtype=jnp.float32), first_factor, 1, 1)
    image = exact_dot(c_zero[:, :K], first_factor, 1, 1)
    moved = exact_dot(c_lag[:, :K], first_factor, 1, 1)
    basis = jnp.pad(spectral_shift * seed, ((0, feature_count - K), (0, 0))) - exact_dot(
        inverse, moved
    )
    image = moved + spectral_shift * image
    for sweep in range(ITERS - 1):
        moved = exact_dot(c_lag, basis)
        basis = spectral_shift * basis - exact_dot(inverse, moved)
        image = moved + spectral_shift * image
    last_factor = small_factor(exact_dot(basis, image, 0, 0))
    shifted = (features - mean_all) * is_valid
    projected = exact_dot(exact_dot(shifted, basis), last_factor, 1, 1)
    return projected[None]


def solution(mesh):
    return jax.shard_map(
        on_device,
        mesh=mesh,
        in_specs=(P("traj", "seg", None, None), P(), P("traj")),
        out_specs=P("traj", "seg", None),
        check_vma=False,
    )
```

```python
import jax
import jax.numpy as jnp
from jax import lax
from jax.experimental import pallas as pl
from jax.experimental.pallas import tpu as pltpu
from jax.sharding import PartitionSpec as P

K = 128
LAG = 10
ITERS = 3
BLOCK = 128
GROUP = 4


exact_mode = lax.Precision.HIGHEST
soft_square = 0.1
ridge_term = 0.01
spectral_shift = 2.0


def exact_dot(left, right, left_axis=1, right_axis=0):
    return lax.dot_general(
        left,
        right,
        (((left_axis,), (right_axis,)), ((), ())),
        precision=exact_mode,
        preferred_element_type=jnp.float32,
    )


def split3(x):
    high = x.astype(jnp.bfloat16)
    rest = x - high.astype(jnp.float32)
    middle = rest.astype(jnp.bfloat16)
    low = (rest - middle.astype(jnp.float32)).astype(jnp.bfloat16)
    return high, middle, low


def inverse_factor(matrix):
    size = matrix.shape[0]
    lane = lax.broadcasted_iota(jnp.int32, (8, size), 1)
    sub = lax.broadcasted_iota(jnp.int32, (8, size), 0)
    rest = matrix.reshape(size // 8, 8, size)
    finished = []
    for start in range(0, size, GROUP):
        top = start % 8
        head = rest[0]
        pivots = [
            [
                jnp.broadcast_to(head[top + a : top + a + 1, start + b : start + b + 1], (8, size))
                if b >= a
                else None
                for b in range(GROUP)
            ]
            for a in range(GROUP)
        ]
        columns = [
            jnp.broadcast_to(rest[:, :, start + a : start + a + 1], rest.shape)
            for a in range(GROUP)
        ]
        rows, inverses = [], []
        for a in range(GROUP):
            row = jnp.broadcast_to(head[top + a : top + a + 1, :], (8, size))
            row = jnp.where((lane >= start) & (lane < start + GROUP), 0.0, row)
            for b in range(a):
                row = row - (pivots[b][a] * inverses[b]) * rows[b]
            inverse = 1.0 / pivots[a][a]
            for b in range(a + 1, GROUP):
                scale = pivots[a][b] * inverse
                for c in range(b, GROUP):
                    pivots[b][c] = pivots[b][c] - scale * pivots[a][c]
            rows.append(jnp.where(lane == start + a, 1.0, row))
            inverses.append(inverse)
        scaled = []
        for a in range(GROUP):
            column = columns[a]
            for b in range(a):
                column = column - scaled[b] * pivots[b][a][None]
            scaled.append(column * inverses[a][None])
        cleared = jnp.where(((lane >= start) & (lane < start + GROUP))[None], 0.0, rest)
        update = scaled[0] * rows[0][None]
        for a in range(1, GROUP):
            update = update + scaled[a] * rows[a][None]
        fresh = cleared - update
        head = jnp.where(sub >= top + GROUP, fresh[0], head)
        for a in range(GROUP):
            head = jnp.where(sub == top + a, rows[a] * jnp.sqrt(inverses[a]), head)
        if top + GROUP == 8:
            finished.append(head)
            rest = fresh[1:] if start + GROUP < size else None
        else:
            rest = jnp.concatenate([head[None], fresh[1:]], axis=0) if len(fresh) > 1 else head[None]
    out = jnp.concatenate(finished, axis=0)
    row_index = lax.broadcasted_iota(jnp.int32, (size, size), 0)
    lane_index = lax.broadcasted_iota(jnp.int32, (size, size), 1)
    return jnp.where(lane_index <= row_index, out, 0.0)


def fold(matrix):
    blocks = matrix.shape[0] // BLOCK
    bands = []
    for i in range(blocks // 2):
        j = blocks - 1 - i
        low = matrix[i * BLOCK : (i + 1) * BLOCK, : (i + 1) * BLOCK]
        high = matrix[j * BLOCK : (j + 1) * BLOCK, : (j + 1) * BLOCK]
        bands.append(jnp.concatenate([low, high], axis=1))
    return jnp.concatenate(bands, axis=0)


def folded_blocks(blocks):
    for i in range(blocks):
        band, begin = (i, 0) if i < blocks // 2 else (blocks - 1 - i, blocks - i)
        for j in range(i + 1):
            yield i, j, band, begin + j


def block_of(i):
    return slice(i * BLOCK, (i + 1) * BLOCK)


def inverse_kernel(tile, folded_ref, left_ref, right_ref, scale_ref, out_ref, first_ref, image_ref, wide):
    size = out_ref.shape[0]
    scale = scale_ref[0, 0]
    row_index = lax.broadcasted_iota(jnp.int32, (BLOCK, BLOCK), 0)
    lane_index = lax.broadcasted_iota(jnp.int32, (BLOCK, BLOCK), 1)
    ridge = jnp.where(row_index == lane_index, ridge_term, 0.0)
    for i, j, band, place in folded_blocks(size // BLOCK):
        between = exact_dot(left_ref[:, block_of(i)], right_ref[:, block_of(j)], 0, 0)
        block = (folded_ref[block_of(band), block_of(place)] + between) * scale
        if i == j:
            out_ref[block_of(i), block_of(i)] = block + ridge
        else:
            out_ref[block_of(i), block_of(j)] = block
            out_ref[block_of(j), block_of(i)] = block.T

    @pl.loop(0, size // BLOCK)
    def _(k):
        here = pl.ds(pl.multiple_of(k * BLOCK, BLOCK), BLOCK)
        factor = inverse_factor(out_ref[here, here])

        @pl.when(k == 0)
        def _():
            first_ref[...] = factor
            image_ref[...] = exact_dot(out_ref[:, :BLOCK], factor, 1, 1)

        pivot = exact_dot(factor, factor, 0, 0)
        row = exact_dot(pivot, out_ref[here, :])
        high, middle, low = split3(row)
        for place, piece in enumerate((high, middle, high, middle, low, high)):
            wide[place * BLOCK : (place + 1) * BLOCK, :] = piece

        @pl.loop(0, size // tile)
        def _(i):
            span = pl.ds(pl.multiple_of(i * tile, tile), tile)
            column = out_ref[span, here]
            h, m, l = split3(column)
            long = jnp.concatenate([h, h, m, m, h, l], axis=1)
            out_ref[span, :] -= jnp.dot(long, wide[...], preferred_element_type=jnp.float32)
            out_ref[span, here] = exact_dot(column, pivot)

        out_ref[here, :] = row
        out_ref[here, here] = -pivot


def negative_inverse(folded, left, right, scale):
    size = left.shape[1]
    vmem, smem = pl.BlockSpec(memory_space=pltpu.VMEM), pl.BlockSpec(memory_space=pltpu.SMEM)
    return pl.pallas_call(
        lambda *refs: inverse_kernel(min(256, size), *refs),
        out_shape=(
            jax.ShapeDtypeStruct((size, size), jnp.float32),
            jax.ShapeDtypeStruct((BLOCK, BLOCK), jnp.float32),
            jax.ShapeDtypeStruct((size, BLOCK), jnp.float32),
        ),
        in_specs=[vmem, vmem, vmem, smem],
        out_specs=(vmem, vmem, vmem),
        scratch_shapes=[pltpu.VMEM((6 * BLOCK, size), jnp.bfloat16)],
        compiler_params=pltpu.CompilerParams(vmem_limit_bytes=40 * 1024 * 1024),
        cost_estimate=pl.CostEstimate(
            flops=120 * size * size * size, bytes_accessed=8 * size * size, transcendentals=0
        ),
        name="negative_inverse",
    )(folded, left, right, scale)


def sweep_kernel(
    tile, folded_ref, left_ref, right_ref, scale_ref, inverse_ref, first_ref, image_ref, shifted_ref,
    out_ref, lag_wide, inverse_wide, vector_wide, vector_tall, moved, basis, image,
):
    size = inverse_ref.shape[0]
    scale = scale_ref[0, 0]

    def put(wide, rows, columns, block):
        for place, piece in enumerate(split3(block)):
            wide[place, rows, columns] = piece

    for i, j, band, place in folded_blocks(size // BLOCK):
        between = exact_dot(left_ref[:, block_of(i)], right_ref[:, block_of(j)], 0, 0)
        block = (folded_ref[block_of(band), block_of(place)] + between) * scale
        put(lag_wide, block_of(i), block_of(j), block)
        if i != j:
            put(lag_wide, block_of(j), block_of(i), block.T)

    @pl.loop(0, size // BLOCK)
    def _(i):
        span = pl.ds(pl.multiple_of(i * BLOCK, BLOCK), BLOCK)
        put(inverse_wide, span, slice(None), inverse_ref[span, :])

    def multiply(wide, vector, sink):
        depth = vector.shape[0]
        high, middle, low = split3(vector)
        vector_wide[:depth, :] = jnp.concatenate([high, middle], axis=1)
        vector_tall[:depth, :] = low
        vector_tall[depth : 2 * depth, :] = high

        @pl.loop(0, size // tile)
        def _(i):
            span = pl.ds(pl.multiple_of(i * tile, tile), tile)
            pair = vector_wide[:depth, :]
            main = jnp.dot(wide[0, span, :depth], pair, preferred_element_type=jnp.float32)
            side = jnp.dot(wide[1, span, :depth], pair, preferred_element_type=jnp.float32)
            ends = jnp.concatenate([wide[0, span, :depth], wide[2, span, :depth]], axis=1)
            last = jnp.dot(ends, vector_tall[: 2 * depth, :], preferred_element_type=jnp.float32)
            both = main + side
            sink(span, both[:, :K] + (both[:, K:] + last))

    def keep_moved(span, value):
        moved[span, :] = value

    def step_basis(span, value):
        basis[span, :] = spectral_shift * basis[span, :] - value

    seed = first_ref[...].T
    basis[...] = jnp.zeros_like(basis)
    basis[:K, :] = seed
    image[...] = image_ref[...]
    for sweep in range(ITERS):
        multiply(lag_wide, seed if sweep == 0 else basis[...], keep_moved)
        image[...] = spectral_shift * image[...] + moved[...]
        multiply(inverse_wide, moved[...], step_basis)
    factor = inverse_factor(exact_dot(basis[...], image[...], 0, 0))
    out_ref[...] = exact_dot(exact_dot(shifted_ref[...], basis[...]), factor, 1, 1)


def sweeps(folded, left, right, scale, inverse, first, image, shifted):
    size = left.shape[1]
    vmem, smem = pl.BlockSpec(memory_space=pltpu.VMEM), pl.BlockSpec(memory_space=pltpu.SMEM)
    return pl.pallas_call(
        lambda *refs: sweep_kernel(min(256, size), *refs),
        out_shape=jax.ShapeDtypeStruct((shifted.shape[0], K), jnp.float32),
        in_specs=[vmem, vmem, vmem, smem, vmem, vmem, vmem, vmem],
        out_specs=vmem,
        scratch_shapes=[
            pltpu.VMEM((3, size, size), jnp.bfloat16),
            pltpu.VMEM((3, size, size), jnp.bfloat16),
            pltpu.VMEM((size, 2 * K), jnp.bfloat16),
            pltpu.VMEM((2 * size, K), jnp.bfloat16),
            pltpu.VMEM((size, K), jnp.float32),
            pltpu.VMEM((size, K), jnp.float32),
            pltpu.VMEM((size, K), jnp.float32),
        ],
        compiler_params=pltpu.CompilerParams(vmem_limit_bytes=48 * 1024 * 1024),
        name="sweeps",
    )(folded, left, right, scale, inverse, first, image, shifted)


def featurize(frames, selection):
    frame_rows, parts, atoms = frames.shape
    offset = exact_dot(jnp.swapaxes(frames, 0, 1).reshape(parts * frame_rows, atoms), selection)
    offset = offset.reshape(parts, frame_rows, -1)
    return jnp.sqrt(jnp.sum(offset * offset, axis=0) + soft_square)


def on_device(coords, pairs, lengths):
    frames = coords[0]
    frame_rows, _, atoms = frames.shape
    feature_count = pairs.shape[1]
    trajs, segs = lax.axis_size("traj"), lax.axis_size("seg")
    devices = trajs * segs
    traj, seg = lax.axis_index("traj"), lax.axis_index("seg")
    me = traj * segs + seg
    length = lengths[0]

    arriving = lax.ppermute(frames[:LAG], "seg", [(i + 1, i) for i in range(segs - 1)])
    atom = jnp.arange(atoms, dtype=jnp.int32)[:, None]
    selection = (atom == pairs[0][None]).astype(jnp.float32) - (atom == pairs[1][None]).astype(
        jnp.float32
    )
    features = featurize(frames, selection)
    lagged = jnp.concatenate([features[LAG:], featurize(arriving, selection)], axis=0)

    frame_index = seg * frame_rows + jnp.arange(frame_rows, dtype=jnp.int32)
    is_valid = (frame_index < length).astype(jnp.float32)[:, None]
    paired = (frame_index + LAG < length).astype(jnp.float32)[:, None]
    count_all = jnp.maximum(jnp.sum(is_valid), 1.0)
    count_pair = jnp.maximum(jnp.sum(paired), 1.0)
    own_all = jnp.sum(features * is_valid, axis=0) / count_all
    own_lead = jnp.sum(features * paired, axis=0) / count_pair
    own_ahead = jnp.sum(lagged * paired, axis=0) / count_pair
    centered = (features - own_all) * is_valid
    lead_rows = (features - own_lead) * paired
    ahead_rows = (lagged - own_ahead) * paired
    gram_zero = exact_dot(centered, centered, 0, 0)
    gram_lag = exact_dot(
        jnp.concatenate([lead_rows, ahead_rows], axis=0),
        jnp.concatenate([ahead_rows, lead_rows], axis=0),
        0,
        0,
    )

    mine = (jnp.arange(devices) == me)[:, None]
    slot_length = jnp.where(
        (jnp.arange(trajs) == traj) & (seg == 0), length.astype(jnp.float32), 0.0
    )
    slot_length = jnp.pad(slot_length[None], ((0, 7), (0, feature_count - trajs)))

    def load_of(gram, slots):
        folded = fold(gram)
        rows = folded.shape[0]
        slots = jnp.concatenate(slots, axis=0)
        wide = -(-slots.size // (rows * BLOCK)) * BLOCK
        taken = wide * rows // feature_count
        slots = jnp.pad(slots, ((0, taken - slots.shape[0]), (0, 0)))
        return jnp.concatenate([folded, slots.reshape(rows, wide)], axis=1)

    def unload(total):
        wide = feature_count + BLOCK
        return total[:, :wide], total[:, wide:].reshape(-1, feature_count)

    first_load = load_of(gram_zero, [jnp.where(mine, own_all[None], 0.0), slot_length])
    first_total = lax.psum(first_load, ("traj", "seg"))
    second_load = load_of(
        gram_lag, [jnp.where(mine, own_lead[None], 0.0), jnp.where(mine, own_ahead[None], 0.0)]
    )
    second_load, first_total = lax.optimization_barrier((second_load, first_total))
    second_total = lax.psum(second_load, ("traj", "seg"))

    folded_zero, slots = unload(first_total)
    all_lengths = slots[devices, :trajs]
    begins = jnp.arange(segs, dtype=jnp.float32)[None] * frame_rows
    counts = jnp.clip(all_lengths[:, None] - begins, 0.0, frame_rows).reshape(devices, 1)
    pair_counts = jnp.clip(all_lengths[:, None] - LAG - begins, 0.0, frame_rows).reshape(devices, 1)
    frames_total, pairs_total = jnp.sum(counts), jnp.sum(pair_counts)
    device_all = slots[:devices]
    mean_all = jnp.sum(device_all * counts, axis=0) / frames_total
    spread_all = device_all - mean_all
    inverse, first_factor, image = negative_inverse(
        folded_zero, spread_all * counts, spread_all, (1.0 / frames_total).reshape(1, 1)
    )

    folded_lag, slots = unload(second_total)
    device_lead, device_ahead = slots[:devices], slots[devices : 2 * devices]
    spread_lead = device_lead - jnp.sum(device_lead * pair_counts, axis=0) / pairs_total
    spread_ahead = device_ahead - jnp.sum(device_ahead * pair_counts, axis=0) / pairs_total
    shifted = (features - mean_all) * is_valid
    projected = sweeps(
        folded_lag,
        jnp.concatenate([spread_lead * pair_counts, spread_ahead * pair_counts], axis=0),
        jnp.concatenate([spread_ahead, spread_lead], axis=0),
        (0.5 / pairs_total).reshape(1, 1),
        inverse,
        first_factor,
        image,
        shifted,
    )
    return projected[None]


def solution(mesh):
    return jax.shard_map(
        on_device,
        mesh=mesh,
        in_specs=(P("traj", "seg", None, None), P(), P("traj")),
        out_specs=P("traj", "seg", None),
        check_vma=False,
    )
```

```python
import jax
import jax.numpy as jnp
from jax import lax
from jax.experimental import pallas as pl
from jax.experimental.pallas import tpu as pltpu
from jax.sharding import PartitionSpec as P

K = 128
LAG = 10
ITERS = 3
BLOCK = 128
GROUP = 4


exact_mode = lax.Precision.HIGHEST
soft_square = 0.1
ridge_term = 0.01
spectral_shift = 2.0


def exact_dot(left, right, left_axis=1, right_axis=0):
    return lax.dot_general(
        left,
        right,
        (((left_axis,), (right_axis,)), ((), ())),
        precision=exact_mode,
        preferred_element_type=jnp.float32,
    )


def split3(x):
    high = x.astype(jnp.bfloat16)
    rest = x - high.astype(jnp.float32)
    middle = rest.astype(jnp.bfloat16)
    low = (rest - middle.astype(jnp.float32)).astype(jnp.bfloat16)
    return high, middle, low


def inverse_factor(matrix):
    size = matrix.shape[0]
    lane = lax.broadcasted_iota(jnp.int32, (8, size), 1)
    sub = lax.broadcasted_iota(jnp.int32, (8, size), 0)
    rest = matrix.reshape(size // 8, 8, size)
    finished = []
    for start in range(0, size, GROUP):
        top = start % 8
        head = rest[0]
        pivots = [
            [
                jnp.broadcast_to(head[top + a : top + a + 1, start + b : start + b + 1], (8, size))
                if b >= a
                else None
                for b in range(GROUP)
            ]
            for a in range(GROUP)
        ]
        columns = [
            jnp.broadcast_to(rest[:, :, start + a : start + a + 1], rest.shape)
            for a in range(GROUP)
        ]
        rows, inverses = [], []
        for a in range(GROUP):
            row = jnp.broadcast_to(head[top + a : top + a + 1, :], (8, size))
            row = jnp.where((lane >= start) & (lane < start + GROUP), 0.0, row)
            for b in range(a):
                row = row - (pivots[b][a] * inverses[b]) * rows[b]
            inverse = 1.0 / pivots[a][a]
            for b in range(a + 1, GROUP):
                scale = pivots[a][b] * inverse
                for c in range(b, GROUP):
                    pivots[b][c] = pivots[b][c] - scale * pivots[a][c]
            rows.append(jnp.where(lane == start + a, 1.0, row))
            inverses.append(inverse)
        scaled = []
        for a in range(GROUP):
            column = columns[a]
            for b in range(a):
                column = column - scaled[b] * pivots[b][a][None]
            scaled.append(column * inverses[a][None])
        cleared = jnp.where(((lane >= start) & (lane < start + GROUP))[None], 0.0, rest)
        update = scaled[0] * rows[0][None]
        for a in range(1, GROUP):
            update = update + scaled[a] * rows[a][None]
        fresh = cleared - update
        head = jnp.where(sub >= top + GROUP, fresh[0], head)
        for a in range(GROUP):
            head = jnp.where(sub == top + a, rows[a] * jnp.sqrt(inverses[a]), head)
        if top + GROUP == 8:
            finished.append(head)
            rest = fresh[1:] if start + GROUP < size else None
        else:
            rest = jnp.concatenate([head[None], fresh[1:]], axis=0) if len(fresh) > 1 else head[None]
    out = jnp.concatenate(finished, axis=0)
    row_index = lax.broadcasted_iota(jnp.int32, (size, size), 0)
    lane_index = lax.broadcasted_iota(jnp.int32, (size, size), 1)
    return jnp.where(lane_index <= row_index, out, 0.0)


def fold(matrix):
    blocks = matrix.shape[0] // BLOCK
    return jnp.concatenate(
        [matrix[block_of(i), block_of(j)] for i in range(blocks) for j in range(i + 1)], axis=0
    )


def folded_blocks(blocks):
    for i in range(blocks):
        for j in range(i + 1):
            yield i, j, i * (i + 1) // 2 + j


def block_of(i):
    return slice(i * BLOCK, (i + 1) * BLOCK)


def inverse_kernel(tile, folded_ref, left_ref, right_ref, scale_ref, out_ref, first_ref, image_ref, wide):
    size = out_ref.shape[0]
    scale = scale_ref[0, 0]
    row_index = lax.broadcasted_iota(jnp.int32, (BLOCK, BLOCK), 0)
    lane_index = lax.broadcasted_iota(jnp.int32, (BLOCK, BLOCK), 1)
    ridge = jnp.where(row_index == lane_index, ridge_term, 0.0)
    for i, j, place in folded_blocks(size // BLOCK):
        between = exact_dot(left_ref[:, block_of(i)], right_ref[:, block_of(j)], 0, 0)
        block = (folded_ref[block_of(place), :] + between) * scale
        if i == j:
            out_ref[block_of(i), block_of(i)] = block + ridge
        else:
            out_ref[block_of(i), block_of(j)] = block
            out_ref[block_of(j), block_of(i)] = block.T

    @pl.loop(0, size // BLOCK)
    def _(k):
        here = pl.ds(pl.multiple_of(k * BLOCK, BLOCK), BLOCK)
        factor = inverse_factor(out_ref[here, here])

        @pl.when(k == 0)
        def _():
            first_ref[...] = factor
            image_ref[...] = exact_dot(out_ref[:, :BLOCK], factor, 1, 1)

        pivot = exact_dot(factor, factor, 0, 0)
        row = exact_dot(pivot, out_ref[here, :])
        high, middle, low = split3(row)
        for place, piece in enumerate((high, middle, high, middle, low, high)):
            wide[place * BLOCK : (place + 1) * BLOCK, :] = piece

        @pl.loop(0, size // tile)
        def _(i):
            span = pl.ds(pl.multiple_of(i * tile, tile), tile)
            column = out_ref[span, here]
            h, m, l = split3(column)
            long = jnp.concatenate([h, h, m, m, h, l], axis=1)
            out_ref[span, :] -= jnp.dot(long, wide[...], preferred_element_type=jnp.float32)
            out_ref[span, here] = exact_dot(column, pivot)

        out_ref[here, :] = row
        out_ref[here, here] = -pivot


def negative_inverse(folded, left, right, scale):
    size = left.shape[1]
    vmem, smem = pl.BlockSpec(memory_space=pltpu.VMEM), pl.BlockSpec(memory_space=pltpu.SMEM)
    return pl.pallas_call(
        lambda *refs: inverse_kernel(min(256, size), *refs),
        out_shape=(
            jax.ShapeDtypeStruct((size, size), jnp.float32),
            jax.ShapeDtypeStruct((BLOCK, BLOCK), jnp.float32),
            jax.ShapeDtypeStruct((size, BLOCK), jnp.float32),
        ),
        in_specs=[vmem, vmem, vmem, smem],
        out_specs=(vmem, vmem, vmem),
        scratch_shapes=[pltpu.VMEM((6 * BLOCK, size), jnp.bfloat16)],
        compiler_params=pltpu.CompilerParams(vmem_limit_bytes=40 * 1024 * 1024),
        cost_estimate=pl.CostEstimate(
            flops=size * size * size, bytes_accessed=8 * size * size, transcendentals=0
        ),
        name="negative_inverse",
    )(folded, left, right, scale)


def sweep_kernel(
    tile, folded_ref, left_ref, right_ref, scale_ref, inverse_ref, first_ref, image_ref, shifted_ref,
    out_ref, lag_wide, inverse_wide, vector_wide, vector_tall, moved, basis, image,
):
    size = inverse_ref.shape[0]
    scale = scale_ref[0, 0]

    def put(wide, rows, columns, block):
        for place, piece in enumerate(split3(block)):
            wide[place, rows, columns] = piece

    for i, j, place in folded_blocks(size // BLOCK):
        between = exact_dot(left_ref[:, block_of(i)], right_ref[:, block_of(j)], 0, 0)
        block = (folded_ref[block_of(place), :] + between) * scale
        put(lag_wide, block_of(i), block_of(j), block)
        if i != j:
            put(lag_wide, block_of(j), block_of(i), block.T)

    @pl.loop(0, size // BLOCK)
    def _(i):
        span = pl.ds(pl.multiple_of(i * BLOCK, BLOCK), BLOCK)
        put(inverse_wide, span, slice(None), inverse_ref[span, :])

    def multiply(wide, vector, sink):
        depth = vector.shape[0]
        high, middle, low = split3(vector)
        vector_wide[:depth, :] = jnp.concatenate([high, middle], axis=1)
        vector_tall[:depth, :] = low
        vector_tall[depth : 2 * depth, :] = high

        @pl.loop(0, size // tile)
        def _(i):
            span = pl.ds(pl.multiple_of(i * tile, tile), tile)
            pair = vector_wide[:depth, :]
            main = jnp.dot(wide[0, span, :depth], pair, preferred_element_type=jnp.float32)
            side = jnp.dot(wide[1, span, :depth], pair, preferred_element_type=jnp.float32)
            ends = jnp.concatenate([wide[0, span, :depth], wide[2, span, :depth]], axis=1)
            last = jnp.dot(ends, vector_tall[: 2 * depth, :], preferred_element_type=jnp.float32)
            both = main + side
            sink(span, both[:, :K] + (both[:, K:] + last))

    def keep_moved(span, value):
        moved[span, :] = value

    def step_basis(span, value):
        basis[span, :] = spectral_shift * basis[span, :] - value

    seed = first_ref[...].T
    basis[...] = jnp.zeros_like(basis)
    basis[:K, :] = seed
    image[...] = image_ref[...]
    for sweep in range(ITERS):
        multiply(lag_wide, seed if sweep == 0 else basis[...], keep_moved)
        image[...] = spectral_shift * image[...] + moved[...]
        multiply(inverse_wide, moved[...], step_basis)
    factor = inverse_factor(exact_dot(basis[...], image[...], 0, 0))
    out_ref[...] = exact_dot(exact_dot(shifted_ref[...], basis[...]), factor, 1, 1)


def sweeps(folded, left, right, scale, inverse, first, image, shifted):
    size = left.shape[1]
    vmem, smem = pl.BlockSpec(memory_space=pltpu.VMEM), pl.BlockSpec(memory_space=pltpu.SMEM)
    return pl.pallas_call(
        lambda *refs: sweep_kernel(min(256, size), *refs),
        out_shape=jax.ShapeDtypeStruct((shifted.shape[0], K), jnp.float32),
        in_specs=[vmem, vmem, vmem, smem, vmem, vmem, vmem, vmem],
        out_specs=vmem,
        scratch_shapes=[
            pltpu.VMEM((3, size, size), jnp.bfloat16),
            pltpu.VMEM((3, size, size), jnp.bfloat16),
            pltpu.VMEM((size, 2 * K), jnp.bfloat16),
            pltpu.VMEM((2 * size, K), jnp.bfloat16),
            pltpu.VMEM((size, K), jnp.float32),
            pltpu.VMEM((size, K), jnp.float32),
            pltpu.VMEM((size, K), jnp.float32),
        ],
        compiler_params=pltpu.CompilerParams(vmem_limit_bytes=48 * 1024 * 1024),
        name="sweeps",
    )(folded, left, right, scale, inverse, first, image, shifted)


def routes(trajs, segs):
    seg_bits = [("seg", 1 << i) for i in range(segs.bit_length() - 1)]
    traj_bits = [("traj", 1 << i) for i in range(trajs.bit_length() - 1)]

    def woven(first, second):
        out = []
        for i in range(max(len(first), len(second))):
            out += first[i : i + 1] + second[i : i + 1]
        return out

    return (
        seg_bits[:1] + woven(seg_bits[1:], traj_bits),
        seg_bits[:1] + woven(traj_bits, seg_bits[1:]),
    )


def sum_kernel(trajs, segs, loads, outs, landings, send_sems, recv_sems):
    traj, seg = lax.axis_index("traj"), lax.axis_index("seg")
    core = seg % 2
    devices = trajs * segs

    def hop(axis, stride):
        bit = ((seg if axis == "seg" else traj) // stride) % 2
        move = stride * (1 - 2 * bit)
        return bit, (move if axis == "traj" else 0 * move), (move if axis == "seg" else 0 * move)

    def steps_of(stream):
        steps = []
        for one, other in zip(*routes(trajs, segs)):
            if stream == 1:
                one, other = other, one
            bit, by_traj, by_seg = (
                (1 - core) * a + core * b for a, b in zip(hop(*one), hop(*other))
            )
            steps.append((bit, (traj + by_traj, seg + by_seg)))
        return steps

    plans = [steps_of(stream) for stream in range(len(loads))]
    count = len(plans[0])

    barrier = pltpu.get_barrier_semaphore()
    for _, partner in plans[0]:
        pl.semaphore_signal(
            barrier, inc=1, device_id=partner, device_id_type=pl.DeviceIdType.MESH
        )
    pl.semaphore_wait(barrier, count)

    lows = [0 * traj for _ in loads]
    kept = [[] for _ in loads]
    flying = [None for _ in loads]

    def send(stream, phase, source, target, partner):
        place = stream * 2 * count + phase
        flying[stream] = pltpu.make_async_remote_copy(
            src_ref=source,
            dst_ref=target,
            send_sem=send_sems.at[place],
            recv_sem=recv_sems.at[place],
            device_id=partner,
            device_id_type=pl.DeviceIdType.MESH,
        )
        flying[stream].start()

    def held(stream, phase):
        half = devices >> (phase + 1)
        bit = plans[stream][phase][0]
        if phase == 0:
            return loads[stream], bit * half, (1 - bit) * half
        begins = devices - 4 * half
        return landings[stream], begins + bit * half, begins + (1 - bit) * half

    def begin(stream, phase):
        if phase < count:
            half = devices >> (phase + 1)
            source, _, give = held(stream, phase)
            kept[stream].append(lows[stream] + plans[stream][phase][0] * half)
            lows[stream] = kept[stream][-1]
            send(
                stream,
                phase,
                source.at[pl.ds(give, half)],
                landings[stream].at[pl.ds(devices - 2 * half, half)],
                plans[stream][phase][1],
            )
        else:
            step = 2 * count - 1 - phase
            span = outs[stream].at[pl.ds(kept[stream][step], devices >> (step + 1))]
            send(stream, phase, span, span, plans[stream][step][1])

    def end(stream, phase):
        flying[stream].wait()
        if phase < count:
            half = devices >> (phase + 1)
            source, keep, _ = held(stream, phase)
            landed = devices - 2 * half
            landing = landings[stream]
            if phase == count - 1:
                outs[stream][lows[stream]] = source[keep] + landing[landed]
            else:

                @pl.loop(0, half)
                def _(i):
                    landing[landed + i] = source[keep + i] + landing[landed + i]

    for phase in range(2 * count + 1):
        for stream in range(len(loads)):
            if phase > 0:
                end(stream, phase - 1)
            if phase < 2 * count:
                begin(stream, phase)


def sum_over_devices(loads, trajs, segs):
    steps = (trajs * segs).bit_length() - 1
    number = len(loads)
    vmem = pl.BlockSpec(memory_space=pltpu.VMEM)

    def body(*refs):
        groups = [refs[i * number : (i + 1) * number] for i in range(3)]
        sum_kernel(trajs, segs, *groups, *refs[3 * number :])

    return pl.pallas_call(
        body,
        out_shape=[jax.ShapeDtypeStruct(load.shape, jnp.float32) for load in loads],
        in_specs=[vmem] * number,
        out_specs=[vmem] * number,
        scratch_shapes=[
            *(pltpu.VMEM((trajs * segs - 1, *load.shape[1:]), jnp.float32) for load in loads),
            pltpu.SemaphoreType.DMA((2 * steps * number,)),
            pltpu.SemaphoreType.DMA((2 * steps * number,)),
        ],
        compiler_params=pltpu.CompilerParams(
            collective_id=0, has_side_effects=True, vmem_limit_bytes=48 * 1024 * 1024
        ),
        cost_estimate=pl.CostEstimate(
            flops=10**9, bytes_accessed=10**7, transcendentals=0
        ),
        name="sum_over_devices",
    )(*loads)


def featurize(frames, selection):
    frame_rows, parts, atoms = frames.shape
    offset = exact_dot(jnp.swapaxes(frames, 0, 1).reshape(parts * frame_rows, atoms), selection)
    offset = offset.reshape(parts, frame_rows, -1)
    return jnp.sqrt(jnp.sum(offset * offset, axis=0) + soft_square)


def on_device(coords, pairs, lengths):
    frames = coords[0]
    frame_rows, _, atoms = frames.shape
    feature_count = pairs.shape[1]
    trajs, segs = lax.axis_size("traj"), lax.axis_size("seg")
    devices = trajs * segs
    traj, seg = lax.axis_index("traj"), lax.axis_index("seg")
    me = traj * segs + seg
    length = lengths[0]

    arriving = lax.ppermute(frames[:LAG], "seg", [(i + 1, i) for i in range(segs - 1)])
    atom = jnp.arange(atoms, dtype=jnp.int32)[:, None]
    selection = (atom == pairs[0][None]).astype(jnp.float32) - (atom == pairs[1][None]).astype(
        jnp.float32
    )
    features = featurize(frames, selection)
    lagged = jnp.concatenate([features[LAG:], featurize(arriving, selection)], axis=0)

    frame_index = seg * frame_rows + jnp.arange(frame_rows, dtype=jnp.int32)
    is_valid = (frame_index < length).astype(jnp.float32)[:, None]
    paired = (frame_index + LAG < length).astype(jnp.float32)[:, None]
    count_all = jnp.maximum(jnp.sum(is_valid), 1.0)
    count_pair = jnp.maximum(jnp.sum(paired), 1.0)
    own_all = jnp.sum(features * is_valid, axis=0) / count_all
    own_lead = jnp.sum(features * paired, axis=0) / count_pair
    own_ahead = jnp.sum(lagged * paired, axis=0) / count_pair
    centered = (features - own_all) * is_valid
    lead_rows = (features - own_lead) * paired
    ahead_rows = (lagged - own_ahead) * paired
    gram_zero = exact_dot(centered, centered, 0, 0)
    gram_lag = exact_dot(
        jnp.concatenate([lead_rows, ahead_rows], axis=0),
        jnp.concatenate([ahead_rows, lead_rows], axis=0),
        0,
        0,
    )

    mine = (jnp.arange(devices) == me)[:, None]
    slot_length = jnp.where(
        (jnp.arange(trajs) == traj) & (seg == 0), length.astype(jnp.float32), 0.0
    )
    slot_length = jnp.pad(slot_length[None], ((0, 7), (0, feature_count - trajs)))

    folded_rows = (feature_count // BLOCK) * (feature_count // BLOCK + 1) // 2 * BLOCK

    def load_of(gram, slots):
        slots = jnp.concatenate(slots, axis=0).reshape(-1, BLOCK)
        loaded = folded_rows + slots.shape[0]
        share = -(-loaded // (8 * devices)) * 8
        slots = jnp.pad(slots, ((0, share * devices - loaded), (0, 0)))
        return jnp.concatenate([fold(gram), slots], axis=0).reshape(devices, share, BLOCK)

    def unload(total):
        total = total.reshape(-1, BLOCK)
        slots = total[folded_rows:]
        per = feature_count // BLOCK
        slots = slots[: slots.shape[0] // per * per]
        return total, slots.reshape(-1, feature_count)

    first_load = load_of(gram_zero, [jnp.where(mine, own_all[None], 0.0), slot_length])
    second_load = load_of(
        gram_lag, [jnp.where(mine, own_lead[None], 0.0), jnp.where(mine, own_ahead[None], 0.0)]
    )
    first_total, second_total = sum_over_devices((first_load, second_load), trajs, segs)

    folded_zero, slots = unload(first_total)
    all_lengths = slots[devices, :trajs]
    begins = jnp.arange(segs, dtype=jnp.float32)[None] * frame_rows
    counts = jnp.clip(all_lengths[:, None] - begins, 0.0, frame_rows).reshape(devices, 1)
    pair_counts = jnp.clip(all_lengths[:, None] - LAG - begins, 0.0, frame_rows).reshape(devices, 1)
    frames_total, pairs_total = jnp.sum(counts), jnp.sum(pair_counts)
    device_all = slots[:devices]
    mean_all = jnp.sum(device_all * counts, axis=0) / frames_total
    spread_all = device_all - mean_all
    inverse, first_factor, image = negative_inverse(
        folded_zero, spread_all * counts, spread_all, (1.0 / frames_total).reshape(1, 1)
    )

    folded_lag, slots = unload(second_total)
    device_lead, device_ahead = slots[:devices], slots[devices : 2 * devices]
    spread_lead = device_lead - jnp.sum(device_lead * pair_counts, axis=0) / pairs_total
    spread_ahead = device_ahead - jnp.sum(device_ahead * pair_counts, axis=0) / pairs_total
    shifted = (features - mean_all) * is_valid
    projected = sweeps(
        folded_lag,
        jnp.concatenate([spread_lead * pair_counts, spread_ahead * pair_counts], axis=0),
        jnp.concatenate([spread_ahead, spread_lead], axis=0),
        (0.5 / pairs_total).reshape(1, 1),
        inverse,
        first_factor,
        image,
        shifted,
    )
    return projected[None]


def solution(mesh):
    return jax.shard_map(
        on_device,
        mesh=mesh,
        in_specs=(P("traj", "seg", None, None), P(), P("traj")),
        out_specs=P("traj", "seg", None),
        check_vma=False,
    )
```

```python
import jax
import jax.numpy as jnp
from jax import lax
from jax.experimental import pallas as pl
from jax.experimental.pallas import tpu as pltpu
from jax.sharding import PartitionSpec as P

K = 128
LAG = 10
ITERS = 3
BLOCK = 128
GROUP = 4


exact_mode = lax.Precision.HIGHEST
soft_square = 0.1
ridge_term = 0.01
spectral_shift = 2.0


def exact_dot(left, right, left_axis=1, right_axis=0):
    return lax.dot_general(
        left,
        right,
        (((left_axis,), (right_axis,)), ((), ())),
        precision=exact_mode,
        preferred_element_type=jnp.float32,
    )


def split3(x):
    high = x.astype(jnp.bfloat16)
    rest = x - high.astype(jnp.float32)
    middle = rest.astype(jnp.bfloat16)
    low = (rest - middle.astype(jnp.float32)).astype(jnp.bfloat16)
    return high, middle, low


def inverse_factor(matrix):
    size = matrix.shape[0]
    lane = lax.broadcasted_iota(jnp.int32, (8, size), 1)
    sub = lax.broadcasted_iota(jnp.int32, (8, size), 0)
    rest = matrix.reshape(size // 8, 8, size)
    finished = []
    for start in range(0, size, GROUP):
        top = start % 8
        head = rest[0]
        pivots = [
            [
                jnp.broadcast_to(head[top + a : top + a + 1, start + b : start + b + 1], (8, size))
                if b >= a
                else None
                for b in range(GROUP)
            ]
            for a in range(GROUP)
        ]
        columns = [
            jnp.broadcast_to(rest[:, :, start + a : start + a + 1], rest.shape)
            for a in range(GROUP)
        ]
        rows, inverses = [], []
        for a in range(GROUP):
            row = jnp.broadcast_to(head[top + a : top + a + 1, :], (8, size))
            row = jnp.where((lane >= start) & (lane < start + GROUP), 0.0, row)
            for b in range(a):
                row = row - (pivots[b][a] * inverses[b]) * rows[b]
            inverse = 1.0 / pivots[a][a]
            for b in range(a + 1, GROUP):
                scale = pivots[a][b] * inverse
                for c in range(b, GROUP):
                    pivots[b][c] = pivots[b][c] - scale * pivots[a][c]
            rows.append(jnp.where(lane == start + a, 1.0, row))
            inverses.append(inverse)
        scaled = []
        for a in range(GROUP):
            column = columns[a]
            for b in range(a):
                column = column - scaled[b] * pivots[b][a][None]
            scaled.append(column * inverses[a][None])
        cleared = jnp.where(((lane >= start) & (lane < start + GROUP))[None], 0.0, rest)
        update = scaled[0] * rows[0][None]
        for a in range(1, GROUP):
            update = update + scaled[a] * rows[a][None]
        fresh = cleared - update
        head = jnp.where(sub >= top + GROUP, fresh[0], head)
        for a in range(GROUP):
            head = jnp.where(sub == top + a, rows[a] * jnp.sqrt(inverses[a]), head)
        if top + GROUP == 8:
            finished.append(head)
            rest = fresh[1:] if start + GROUP < size else None
        else:
            rest = jnp.concatenate([head[None], fresh[1:]], axis=0) if len(fresh) > 1 else head[None]
    out = jnp.concatenate(finished, axis=0)
    row_index = lax.broadcasted_iota(jnp.int32, (size, size), 0)
    lane_index = lax.broadcasted_iota(jnp.int32, (size, size), 1)
    return jnp.where(lane_index <= row_index, out, 0.0)


def folded_blocks(blocks):
    for i in range(blocks):
        for j in range(i + 1):
            yield i, j, i * (i + 1) // 2 + j


def block_of(i):
    return slice(i * BLOCK, (i + 1) * BLOCK)


def inverse_kernel(tile, folded_ref, left_ref, right_ref, scale_ref, out_ref, first_ref, image_ref, wide):
    size = out_ref.shape[0]
    scale = scale_ref[0, 0]
    row_index = lax.broadcasted_iota(jnp.int32, (BLOCK, BLOCK), 0)
    lane_index = lax.broadcasted_iota(jnp.int32, (BLOCK, BLOCK), 1)
    ridge = jnp.where(row_index == lane_index, ridge_term, 0.0)
    for i, j, place in folded_blocks(size // BLOCK):
        between = exact_dot(left_ref[:, block_of(i)], right_ref[:, block_of(j)], 0, 0)
        block = (folded_ref[block_of(place), :] + between) * scale
        if i == j:
            out_ref[block_of(i), block_of(i)] = block + ridge
        else:
            out_ref[block_of(i), block_of(j)] = block
            out_ref[block_of(j), block_of(i)] = block.T

    @pl.loop(0, size // BLOCK)
    def _(k):
        here = pl.ds(pl.multiple_of(k * BLOCK, BLOCK), BLOCK)
        factor = inverse_factor(out_ref[here, here])

        @pl.when(k == 0)
        def _():
            first_ref[...] = factor
            image_ref[...] = exact_dot(out_ref[:, :BLOCK], factor, 1, 1)

        pivot = exact_dot(factor, factor, 0, 0)
        row = exact_dot(pivot, out_ref[here, :])
        high, middle, low = split3(row)
        for place, piece in enumerate((high, middle, high, middle, low, high)):
            wide[place * BLOCK : (place + 1) * BLOCK, :] = piece

        @pl.loop(0, size // tile)
        def _(i):
            span = pl.ds(pl.multiple_of(i * tile, tile), tile)
            column = out_ref[span, here]
            h, m, l = split3(column)
            long = jnp.concatenate([h, h, m, m, h, l], axis=1)
            out_ref[span, :] -= jnp.dot(long, wide[...], preferred_element_type=jnp.float32)
            out_ref[span, here] = exact_dot(column, pivot)

        out_ref[here, :] = row
        out_ref[here, here] = -pivot


def negative_inverse(folded, left, right, scale):
    size = left.shape[1]
    vmem, smem = pl.BlockSpec(memory_space=pltpu.VMEM), pl.BlockSpec(memory_space=pltpu.SMEM)
    return pl.pallas_call(
        lambda *refs: inverse_kernel(min(256, size), *refs),
        out_shape=(
            jax.ShapeDtypeStruct((size, size), jnp.float32),
            jax.ShapeDtypeStruct((BLOCK, BLOCK), jnp.float32),
            jax.ShapeDtypeStruct((size, BLOCK), jnp.float32),
        ),
        in_specs=[vmem, vmem, vmem, smem],
        out_specs=(vmem, vmem, vmem),
        scratch_shapes=[pltpu.VMEM((6 * BLOCK, size), jnp.bfloat16)],
        compiler_params=pltpu.CompilerParams(vmem_limit_bytes=40 * 1024 * 1024),
        cost_estimate=pl.CostEstimate(
            flops=size * size * size, bytes_accessed=8 * size * size, transcendentals=0
        ),
        name="negative_inverse",
    )(folded, left, right, scale)


def sweep_kernel(
    tile, folded_ref, left_ref, right_ref, scale_ref, inverse_ref, first_ref, image_ref, shifted_ref,
    out_ref, lag_wide, inverse_wide, vector_wide, vector_tall, moved, basis, image,
):
    size = inverse_ref.shape[0]
    scale = scale_ref[0, 0]

    def put(wide, rows, columns, block):
        for place, piece in enumerate(split3(block)):
            wide[place, rows, columns] = piece

    for i, j, place in folded_blocks(size // BLOCK):
        between = exact_dot(left_ref[:, block_of(i)], right_ref[:, block_of(j)], 0, 0)
        block = (folded_ref[block_of(place), :] + between) * scale
        put(lag_wide, block_of(i), block_of(j), block)
        if i != j:
            put(lag_wide, block_of(j), block_of(i), block.T)

    @pl.loop(0, size // BLOCK)
    def _(i):
        span = pl.ds(pl.multiple_of(i * BLOCK, BLOCK), BLOCK)
        put(inverse_wide, span, slice(None), inverse_ref[span, :])

    def multiply(wide, vector, sink):
        depth = vector.shape[0]
        high, middle, low = split3(vector)
        vector_wide[:depth, :] = jnp.concatenate([high, middle], axis=1)
        vector_tall[:depth, :] = low
        vector_tall[depth : 2 * depth, :] = high

        @pl.loop(0, size // tile)
        def _(i):
            span = pl.ds(pl.multiple_of(i * tile, tile), tile)
            pair = vector_wide[:depth, :]
            main = jnp.dot(wide[0, span, :depth], pair, preferred_element_type=jnp.float32)
            side = jnp.dot(wide[1, span, :depth], pair, preferred_element_type=jnp.float32)
            ends = jnp.concatenate([wide[0, span, :depth], wide[2, span, :depth]], axis=1)
            last = jnp.dot(ends, vector_tall[: 2 * depth, :], preferred_element_type=jnp.float32)
            both = main + side
            sink(span, both[:, :K] + (both[:, K:] + last))

    def keep_moved(span, value):
        moved[span, :] = value

    def step_basis(span, value):
        basis[span, :] = spectral_shift * basis[span, :] - value

    seed = first_ref[...].T
    basis[...] = jnp.zeros_like(basis)
    basis[:K, :] = seed
    image[...] = image_ref[...]
    for sweep in range(ITERS):
        multiply(lag_wide, seed if sweep == 0 else basis[...], keep_moved)
        image[...] = spectral_shift * image[...] + moved[...]
        multiply(inverse_wide, moved[...], step_basis)
    factor = inverse_factor(exact_dot(basis[...], image[...], 0, 0))
    out_ref[...] = exact_dot(exact_dot(shifted_ref[...], basis[...]), factor, 1, 1)


def sweeps(folded, left, right, scale, inverse, first, image, shifted):
    size = left.shape[1]
    vmem, smem = pl.BlockSpec(memory_space=pltpu.VMEM), pl.BlockSpec(memory_space=pltpu.SMEM)
    return pl.pallas_call(
        lambda *refs: sweep_kernel(min(256, size), *refs),
        out_shape=jax.ShapeDtypeStruct((shifted.shape[0], K), jnp.float32),
        in_specs=[vmem, vmem, vmem, smem, vmem, vmem, vmem, vmem],
        out_specs=vmem,
        scratch_shapes=[
            pltpu.VMEM((3, size, size), jnp.bfloat16),
            pltpu.VMEM((3, size, size), jnp.bfloat16),
            pltpu.VMEM((size, 2 * K), jnp.bfloat16),
            pltpu.VMEM((2 * size, K), jnp.bfloat16),
            pltpu.VMEM((size, K), jnp.float32),
            pltpu.VMEM((size, K), jnp.float32),
            pltpu.VMEM((size, K), jnp.float32),
        ],
        compiler_params=pltpu.CompilerParams(vmem_limit_bytes=48 * 1024 * 1024),
        name="sweeps",
    )(folded, left, right, scale, inverse, first, image, shifted)


def gram_kernel(zero_ref, lead_ref, ahead_ref, zero_slots, lag_slots, zero_out, lag_out):
    size = zero_ref.shape[1]
    left = jnp.concatenate([lead_ref[...], ahead_ref[...]], axis=0)
    right = jnp.concatenate([ahead_ref[...], lead_ref[...]], axis=0)
    zero = zero_ref[...]
    for i in range(size // BLOCK):
        upto = (i + 1) * BLOCK
        band_zero = exact_dot(zero[:, block_of(i)], zero[:, :upto], 0, 0)
        band_lag = exact_dot(left[:, block_of(i)], right[:, :upto], 0, 0)
        for j in range(i + 1):
            place = block_of(i * (i + 1) // 2 + j)
            zero_out[place, :] = band_zero[:, block_of(j)]
            lag_out[place, :] = band_lag[:, block_of(j)]
    for slots, out in ((zero_slots, zero_out), (lag_slots, lag_out)):
        out[out.shape[0] - slots.shape[0] :, :] = slots[...]


def grams(zero, lead, ahead, zero_slots, lag_slots):
    blocks = zero.shape[1] // BLOCK
    folded = blocks * (blocks + 1) // 2 * BLOCK
    vmem = pl.BlockSpec(memory_space=pltpu.VMEM)
    return pl.pallas_call(
        gram_kernel,
        out_shape=[
            jax.ShapeDtypeStruct((folded + slots.shape[0], BLOCK), jnp.float32)
            for slots in (zero_slots, lag_slots)
        ],
        in_specs=[vmem] * 5,
        out_specs=[vmem] * 2,
        compiler_params=pltpu.CompilerParams(vmem_limit_bytes=40 * 1024 * 1024),
        name="grams",
    )(zero, lead, ahead, zero_slots, lag_slots)


def routes(trajs, segs):
    seg_bits = [("seg", 1 << i) for i in range(segs.bit_length() - 1)]
    traj_bits = [("traj", 1 << i) for i in range(trajs.bit_length() - 1)]

    def woven(first, second):
        out = []
        for i in range(max(len(first), len(second))):
            out += first[i : i + 1] + second[i : i + 1]
        return out

    return (
        seg_bits[:1] + woven(seg_bits[1:], traj_bits),
        seg_bits[:1] + woven(traj_bits, seg_bits[1:]),
    )


def sum_kernel(trajs, segs, loads, outs, landings, send_sems, recv_sems):
    traj, seg = lax.axis_index("traj"), lax.axis_index("seg")
    core = seg % 2
    devices = trajs * segs

    def hop(axis, stride):
        bit = ((seg if axis == "seg" else traj) // stride) % 2
        move = stride * (1 - 2 * bit)
        return bit, (move if axis == "traj" else 0 * move), (move if axis == "seg" else 0 * move)

    def steps_of(stream):
        steps = []
        for one, other in zip(*routes(trajs, segs)):
            if stream == 1:
                one, other = other, one
            bit, by_traj, by_seg = (
                (1 - core) * a + core * b for a, b in zip(hop(*one), hop(*other))
            )
            steps.append((bit, (traj + by_traj, seg + by_seg)))
        return steps

    plans = [steps_of(stream) for stream in range(len(loads))]
    count = len(plans[0])

    barrier = pltpu.get_barrier_semaphore()
    for _, partner in plans[0]:
        pl.semaphore_signal(
            barrier, inc=1, device_id=partner, device_id_type=pl.DeviceIdType.MESH
        )
    pl.semaphore_wait(barrier, count)

    lows = [0 * traj for _ in loads]
    kept = [[] for _ in loads]
    flying = [None for _ in loads]

    def send(stream, phase, source, target, partner):
        place = stream * 2 * count + phase
        flying[stream] = pltpu.make_async_remote_copy(
            src_ref=source,
            dst_ref=target,
            send_sem=send_sems.at[place],
            recv_sem=recv_sems.at[place],
            device_id=partner,
            device_id_type=pl.DeviceIdType.MESH,
        )
        flying[stream].start()

    def held(stream, phase):
        half = devices >> (phase + 1)
        bit = plans[stream][phase][0]
        if phase == 0:
            return loads[stream], bit * half, (1 - bit) * half
        begins = devices - 4 * half
        return landings[stream], begins + bit * half, begins + (1 - bit) * half

    def begin(stream, phase):
        if phase < count:
            half = devices >> (phase + 1)
            source, _, give = held(stream, phase)
            kept[stream].append(lows[stream] + plans[stream][phase][0] * half)
            lows[stream] = kept[stream][-1]
            send(
                stream,
                phase,
                source.at[pl.ds(give, half)],
                landings[stream].at[pl.ds(devices - 2 * half, half)],
                plans[stream][phase][1],
            )
        else:
            step = 2 * count - 1 - phase
            span = outs[stream].at[pl.ds(kept[stream][step], devices >> (step + 1))]
            send(stream, phase, span, span, plans[stream][step][1])

    def end(stream, phase):
        flying[stream].wait()
        if phase < count:
            half = devices >> (phase + 1)
            source, keep, _ = held(stream, phase)
            landed = devices - 2 * half
            landing = landings[stream]
            if phase == count - 1:
                outs[stream][lows[stream]] = source[keep] + landing[landed]
            else:

                @pl.loop(0, half)
                def _(i):
                    landing[landed + i] = source[keep + i] + landing[landed + i]

    for phase in range(2 * count + 1):
        for stream in range(len(loads)):
            if phase > 0:
                end(stream, phase - 1)
            if phase < 2 * count:
                begin(stream, phase)


def sum_over_devices(loads, trajs, segs):
    steps = (trajs * segs).bit_length() - 1
    number = len(loads)
    vmem = pl.BlockSpec(memory_space=pltpu.VMEM)

    def body(*refs):
        groups = [refs[i * number : (i + 1) * number] for i in range(3)]
        sum_kernel(trajs, segs, *groups, *refs[3 * number :])

    return pl.pallas_call(
        body,
        out_shape=[jax.ShapeDtypeStruct(load.shape, jnp.float32) for load in loads],
        in_specs=[vmem] * number,
        out_specs=[vmem] * number,
        scratch_shapes=[
            *(pltpu.VMEM((trajs * segs - 1, *load.shape[1:]), jnp.float32) for load in loads),
            pltpu.SemaphoreType.DMA((2 * steps * number,)),
            pltpu.SemaphoreType.DMA((2 * steps * number,)),
        ],
        compiler_params=pltpu.CompilerParams(
            collective_id=0, has_side_effects=True, vmem_limit_bytes=48 * 1024 * 1024
        ),
        cost_estimate=pl.CostEstimate(
            flops=10**9, bytes_accessed=10**7, transcendentals=0
        ),
        name="sum_over_devices",
    )(*loads)


def featurize(frames, selection):
    frame_rows, parts, atoms = frames.shape
    offset = exact_dot(jnp.swapaxes(frames, 0, 1).reshape(parts * frame_rows, atoms), selection)
    offset = offset.reshape(parts, frame_rows, -1)
    return jnp.sqrt(jnp.sum(offset * offset, axis=0) + soft_square)


def on_device(coords, pairs, lengths):
    frames = coords[0]
    frame_rows, _, atoms = frames.shape
    feature_count = pairs.shape[1]
    trajs, segs = lax.axis_size("traj"), lax.axis_size("seg")
    devices = trajs * segs
    traj, seg = lax.axis_index("traj"), lax.axis_index("seg")
    me = traj * segs + seg
    length = lengths[0]

    arriving = lax.ppermute(frames[:LAG], "seg", [(i + 1, i) for i in range(segs - 1)])
    atom = jnp.arange(atoms, dtype=jnp.int32)[:, None]
    selection = (atom == pairs[0][None]).astype(jnp.float32) - (atom == pairs[1][None]).astype(
        jnp.float32
    )
    features = featurize(frames, selection)
    lagged = jnp.concatenate([features[LAG:], featurize(arriving, selection)], axis=0)

    frame_index = seg * frame_rows + jnp.arange(frame_rows, dtype=jnp.int32)
    is_valid = (frame_index < length).astype(jnp.float32)[:, None]
    paired = (frame_index + LAG < length).astype(jnp.float32)[:, None]
    count_all = jnp.maximum(jnp.sum(is_valid), 1.0)
    count_pair = jnp.maximum(jnp.sum(paired), 1.0)
    own_all = jnp.sum(features * is_valid, axis=0) / count_all
    own_lead = jnp.sum(features * paired, axis=0) / count_pair
    own_ahead = jnp.sum(lagged * paired, axis=0) / count_pair
    centered = (features - own_all) * is_valid
    lead_rows = (features - own_lead) * paired
    ahead_rows = (lagged - own_ahead) * paired
    mine = (jnp.arange(devices) == me)[:, None]
    slot_length = jnp.where(
        (jnp.arange(trajs) == traj) & (seg == 0), length.astype(jnp.float32), 0.0
    )
    slot_length = jnp.pad(slot_length[None], ((0, 7), (0, feature_count - trajs)))

    folded_rows = (feature_count // BLOCK) * (feature_count // BLOCK + 1) // 2 * BLOCK

    def padded(slots):
        slots = jnp.concatenate(slots, axis=0).reshape(-1, BLOCK)
        loaded = folded_rows + slots.shape[0]
        share = -(-loaded // (8 * devices)) * 8
        return jnp.pad(slots, ((0, share * devices - loaded), (0, 0)))

    def unload(total):
        total = total.reshape(-1, BLOCK)
        slots = total[folded_rows:]
        per = feature_count // BLOCK
        slots = slots[: slots.shape[0] // per * per]
        return total, slots.reshape(-1, feature_count)

    loads = grams(
        centered,
        lead_rows,
        ahead_rows,
        padded([jnp.where(mine, own_all[None], 0.0), slot_length]),
        padded(
            [jnp.where(mine, own_lead[None], 0.0), jnp.where(mine, own_ahead[None], 0.0)]
        ),
    )
    loads = [load.reshape(devices, -1, BLOCK) for load in loads]
    first_total, second_total = sum_over_devices(loads, trajs, segs)

    folded_zero, slots = unload(first_total)
    all_lengths = slots[devices, :trajs]
    begins = jnp.arange(segs, dtype=jnp.float32)[None] * frame_rows
    counts = jnp.clip(all_lengths[:, None] - begins, 0.0, frame_rows).reshape(devices, 1)
    pair_counts = jnp.clip(all_lengths[:, None] - LAG - begins, 0.0, frame_rows).reshape(devices, 1)
    frames_total, pairs_total = jnp.sum(counts), jnp.sum(pair_counts)
    device_all = slots[:devices]
    mean_all = jnp.sum(device_all * counts, axis=0) / frames_total
    spread_all = device_all - mean_all
    inverse, first_factor, image = negative_inverse(
        folded_zero, spread_all * counts, spread_all, (1.0 / frames_total).reshape(1, 1)
    )

    folded_lag, slots = unload(second_total)
    device_lead, device_ahead = slots[:devices], slots[devices : 2 * devices]
    spread_lead = device_lead - jnp.sum(device_lead * pair_counts, axis=0) / pairs_total
    spread_ahead = device_ahead - jnp.sum(device_ahead * pair_counts, axis=0) / pairs_total
    shifted = (features - mean_all) * is_valid
    projected = sweeps(
        folded_lag,
        jnp.concatenate([spread_lead * pair_counts, spread_ahead * pair_counts], axis=0),
        jnp.concatenate([spread_ahead, spread_lead], axis=0),
        (0.5 / pairs_total).reshape(1, 1),
        inverse,
        first_factor,
        image,
        shifted,
    )
    return projected[None]


def solution(mesh):
    return jax.shard_map(
        on_device,
        mesh=mesh,
        in_specs=(P("traj", "seg", None, None), P(), P("traj")),
        out_specs=P("traj", "seg", None),
        check_vma=False,
    )
```

```python
import jax
import jax.numpy as jnp
from jax import lax
from jax.experimental import pallas as pl
from jax.experimental.pallas import tpu as pltpu
from jax.sharding import PartitionSpec as P

K = 128
LAG = 10
ITERS = 3
BLOCK = 128
GROUP = 4


exact_mode = lax.Precision.HIGHEST
soft_square = 0.1
ridge_term = 0.01
spectral_shift = 2.0


def exact_dot(left, right, left_axis=1, right_axis=0):
    return lax.dot_general(
        left,
        right,
        (((left_axis,), (right_axis,)), ((), ())),
        precision=exact_mode,
        preferred_element_type=jnp.float32,
    )


def split3(x):
    high = x.astype(jnp.bfloat16)
    rest = x - high.astype(jnp.float32)
    middle = rest.astype(jnp.bfloat16)
    low = (rest - middle.astype(jnp.float32)).astype(jnp.bfloat16)
    return high, middle, low


def inverse_factor(matrix):
    size = matrix.shape[0]
    lane = lax.broadcasted_iota(jnp.int32, (8, size), 1)
    sub = lax.broadcasted_iota(jnp.int32, (8, size), 0)
    rest = matrix.reshape(size // 8, 8, size)
    finished = []
    for start in range(0, size, GROUP):
        top = start % 8
        head = rest[0]
        pivots = [
            [
                jnp.broadcast_to(head[top + a : top + a + 1, start + b : start + b + 1], (8, size))
                if b >= a
                else None
                for b in range(GROUP)
            ]
            for a in range(GROUP)
        ]
        columns = [
            jnp.broadcast_to(rest[:, :, start + a : start + a + 1], rest.shape)
            for a in range(GROUP)
        ]
        rows, inverses = [], []
        for a in range(GROUP):
            row = jnp.broadcast_to(head[top + a : top + a + 1, :], (8, size))
            row = jnp.where((lane >= start) & (lane < start + GROUP), 0.0, row)
            for b in range(a):
                row = row - (pivots[b][a] * inverses[b]) * rows[b]
            inverse = 1.0 / pivots[a][a]
            for b in range(a + 1, GROUP):
                scale = pivots[a][b] * inverse
                for c in range(b, GROUP):
                    pivots[b][c] = pivots[b][c] - scale * pivots[a][c]
            rows.append(jnp.where(lane == start + a, 1.0, row))
            inverses.append(inverse)
        scaled = []
        for a in range(GROUP):
            column = columns[a]
            for b in range(a):
                column = column - scaled[b] * pivots[b][a][None]
            scaled.append(column * inverses[a][None])
        cleared = jnp.where(((lane >= start) & (lane < start + GROUP))[None], 0.0, rest)
        update = scaled[0] * rows[0][None]
        for a in range(1, GROUP):
            update = update + scaled[a] * rows[a][None]
        fresh = cleared - update
        head = jnp.where(sub >= top + GROUP, fresh[0], head)
        for a in range(GROUP):
            head = jnp.where(sub == top + a, rows[a] * jnp.sqrt(inverses[a]), head)
        if top + GROUP == 8:
            finished.append(head)
            rest = fresh[1:] if start + GROUP < size else None
        else:
            rest = jnp.concatenate([head[None], fresh[1:]], axis=0) if len(fresh) > 1 else head[None]
    out = jnp.concatenate(finished, axis=0)
    row_index = lax.broadcasted_iota(jnp.int32, (size, size), 0)
    lane_index = lax.broadcasted_iota(jnp.int32, (size, size), 1)
    return jnp.where(lane_index <= row_index, out, 0.0)


def folded_blocks(blocks):
    for i in range(blocks):
        for j in range(i + 1):
            yield i, j, i * (i + 1) // 2 + j


def block_of(i):
    return slice(i * BLOCK, (i + 1) * BLOCK)


def inverse_kernel(tile, folded_ref, left_ref, right_ref, scale_ref, out_ref, first_ref, image_ref, wide, held):
    size = out_ref.shape[0]
    scale = scale_ref[0, 0]
    row_index = lax.broadcasted_iota(jnp.int32, (BLOCK, BLOCK), 0)
    lane_index = lax.broadcasted_iota(jnp.int32, (BLOCK, BLOCK), 1)
    ridge = jnp.where(row_index == lane_index, ridge_term, 0.0)
    for i, j, place in folded_blocks(size // BLOCK):
        between = exact_dot(left_ref[:, block_of(i)], right_ref[:, block_of(j)], 0, 0)
        block = (folded_ref[block_of(place), :] + between) * scale
        if i == j:
            out_ref[block_of(i), block_of(i)] = block + ridge
        else:
            out_ref[block_of(i), block_of(j)] = block
            out_ref[block_of(j), block_of(i)] = block.T

    first = inverse_factor(out_ref[:BLOCK, :BLOCK])
    first_ref[...] = first
    held[...] = first
    image_ref[...] = exact_dot(out_ref[:, :BLOCK], first, 1, 1)
    last = size // BLOCK - 1

    def long_of(column):
        h, m, l = split3(column)
        return jnp.concatenate([h, h, m, m, h, l], axis=1)

    @pl.loop(0, size // BLOCK)
    def _(k):
        here = pl.ds(pl.multiple_of(k * BLOCK, BLOCK), BLOCK)
        then = pl.ds(pl.multiple_of(jnp.minimum(k + 1, last) * BLOCK, BLOCK), BLOCK)
        factor = held[...]
        pivot = exact_dot(factor, factor, 0, 0)
        row = exact_dot(pivot, out_ref[here, :])
        high, middle, low = split3(row)
        for place, piece in enumerate((high, middle, high, middle, low, high)):
            wide[place * BLOCK : (place + 1) * BLOCK, :] = piece
        ahead = out_ref[then, then] - jnp.dot(
            long_of(out_ref[then, here]), wide[:, then], preferred_element_type=jnp.float32
        )
        held[...] = inverse_factor(ahead)
        for i in range(size // tile):
            span = slice(i * tile, (i + 1) * tile)
            column = out_ref[span, here]
            out_ref[span, :] -= jnp.dot(
                long_of(column), wide[...], preferred_element_type=jnp.float32
            )
            out_ref[span, here] = exact_dot(column, pivot)
        out_ref[here, :] = row
        out_ref[here, here] = -pivot


def negative_inverse(folded, left, right, scale):
    size = left.shape[1]
    vmem, smem = pl.BlockSpec(memory_space=pltpu.VMEM), pl.BlockSpec(memory_space=pltpu.SMEM)
    return pl.pallas_call(
        lambda *refs: inverse_kernel(min(256, size), *refs),
        out_shape=(
            jax.ShapeDtypeStruct((size, size), jnp.float32),
            jax.ShapeDtypeStruct((BLOCK, BLOCK), jnp.float32),
            jax.ShapeDtypeStruct((size, BLOCK), jnp.float32),
        ),
        in_specs=[vmem, vmem, vmem, smem],
        out_specs=(vmem, vmem, vmem),
        scratch_shapes=[
            pltpu.VMEM((6 * BLOCK, size), jnp.bfloat16),
            pltpu.VMEM((BLOCK, BLOCK), jnp.float32),
        ],
        compiler_params=pltpu.CompilerParams(vmem_limit_bytes=40 * 1024 * 1024),
        cost_estimate=pl.CostEstimate(
            flops=size * size * size, bytes_accessed=8 * size * size, transcendentals=0
        ),
        name="negative_inverse",
    )(folded, left, right, scale)


def sweep_kernel(
    tile, folded_ref, left_ref, right_ref, scale_ref, inverse_ref, first_ref, image_ref, shifted_ref,
    out_ref, lag_wide, inverse_wide, vector_wide, vector_tall, moved, basis, image,
):
    size = inverse_ref.shape[0]
    scale = scale_ref[0, 0]

    def put(wide, rows, columns, block):
        for place, piece in enumerate(split3(block)):
            wide[place, rows, columns] = piece

    for i, j, place in folded_blocks(size // BLOCK):
        between = exact_dot(left_ref[:, block_of(i)], right_ref[:, block_of(j)], 0, 0)
        block = (folded_ref[block_of(place), :] + between) * scale
        put(lag_wide, block_of(i), block_of(j), block)
        if i != j:
            put(lag_wide, block_of(j), block_of(i), block.T)

    @pl.loop(0, size // BLOCK)
    def _(i):
        span = pl.ds(pl.multiple_of(i * BLOCK, BLOCK), BLOCK)
        put(inverse_wide, span, slice(None), inverse_ref[span, :])

    def multiply(wide, vector, sink):
        depth = vector.shape[0]
        high, middle, low = split3(vector)
        vector_wide[:depth, :] = jnp.concatenate([high, middle], axis=1)
        vector_tall[:depth, :] = low
        vector_tall[depth : 2 * depth, :] = high

        @pl.loop(0, size // tile)
        def _(i):
            span = pl.ds(pl.multiple_of(i * tile, tile), tile)
            pair = vector_wide[:depth, :]
            main = jnp.dot(wide[0, span, :depth], pair, preferred_element_type=jnp.float32)
            side = jnp.dot(wide[1, span, :depth], pair, preferred_element_type=jnp.float32)
            ends = jnp.concatenate([wide[0, span, :depth], wide[2, span, :depth]], axis=1)
            last = jnp.dot(ends, vector_tall[: 2 * depth, :], preferred_element_type=jnp.float32)
            both = main + side
            sink(span, both[:, :K] + (both[:, K:] + last))

    def keep_moved(span, value):
        moved[span, :] = value

    def step_basis(span, value):
        basis[span, :] = spectral_shift * basis[span, :] - value

    seed = first_ref[...].T
    basis[...] = jnp.zeros_like(basis)
    basis[:K, :] = seed
    image[...] = image_ref[...]
    for sweep in range(ITERS):
        multiply(lag_wide, seed if sweep == 0 else basis[...], keep_moved)
        image[...] = spectral_shift * image[...] + moved[...]
        multiply(inverse_wide, moved[...], step_basis)
    factor = inverse_factor(exact_dot(basis[...], image[...], 0, 0))
    out_ref[...] = exact_dot(exact_dot(shifted_ref[...], basis[...]), factor, 1, 1)


def sweeps(folded, left, right, scale, inverse, first, image, shifted):
    size = left.shape[1]
    vmem, smem = pl.BlockSpec(memory_space=pltpu.VMEM), pl.BlockSpec(memory_space=pltpu.SMEM)
    return pl.pallas_call(
        lambda *refs: sweep_kernel(min(256, size), *refs),
        out_shape=jax.ShapeDtypeStruct((shifted.shape[0], K), jnp.float32),
        in_specs=[vmem, vmem, vmem, smem, vmem, vmem, vmem, vmem],
        out_specs=vmem,
        scratch_shapes=[
            pltpu.VMEM((3, size, size), jnp.bfloat16),
            pltpu.VMEM((3, size, size), jnp.bfloat16),
            pltpu.VMEM((size, 2 * K), jnp.bfloat16),
            pltpu.VMEM((2 * size, K), jnp.bfloat16),
            pltpu.VMEM((size, K), jnp.float32),
            pltpu.VMEM((size, K), jnp.float32),
            pltpu.VMEM((size, K), jnp.float32),
        ],
        compiler_params=pltpu.CompilerParams(vmem_limit_bytes=48 * 1024 * 1024),
        name="sweeps",
    )(folded, left, right, scale, inverse, first, image, shifted)


def gram_kernel(zero_ref, lead_ref, ahead_ref, zero_slots, lag_slots, zero_out, lag_out):
    size = zero_ref.shape[1]
    left = jnp.concatenate([lead_ref[...], ahead_ref[...]], axis=0)
    right = jnp.concatenate([ahead_ref[...], lead_ref[...]], axis=0)
    zero = zero_ref[...]
    for i in range(size // BLOCK):
        upto = (i + 1) * BLOCK
        band_zero = exact_dot(zero[:, block_of(i)], zero[:, :upto], 0, 0)
        band_lag = exact_dot(left[:, block_of(i)], right[:, :upto], 0, 0)
        for j in range(i + 1):
            place = block_of(i * (i + 1) // 2 + j)
            zero_out[place, :] = band_zero[:, block_of(j)]
            lag_out[place, :] = band_lag[:, block_of(j)]
    for slots, out in ((zero_slots, zero_out), (lag_slots, lag_out)):
        out[out.shape[0] - slots.shape[0] :, :] = slots[...]


def grams(zero, lead, ahead, zero_slots, lag_slots):
    blocks = zero.shape[1] // BLOCK
    folded = blocks * (blocks + 1) // 2 * BLOCK
    vmem = pl.BlockSpec(memory_space=pltpu.VMEM)
    return pl.pallas_call(
        gram_kernel,
        out_shape=[
            jax.ShapeDtypeStruct((folded + slots.shape[0], BLOCK), jnp.float32)
            for slots in (zero_slots, lag_slots)
        ],
        in_specs=[vmem] * 5,
        out_specs=[vmem] * 2,
        compiler_params=pltpu.CompilerParams(vmem_limit_bytes=40 * 1024 * 1024),
        name="grams",
    )(zero, lead, ahead, zero_slots, lag_slots)


def routes(trajs, segs):
    seg_bits = [("seg", 1 << i) for i in range(segs.bit_length() - 1)]
    traj_bits = [("traj", 1 << i) for i in range(trajs.bit_length() - 1)]

    def woven(first, second):
        out = []
        for i in range(max(len(first), len(second))):
            out += first[i : i + 1] + second[i : i + 1]
        return out

    return (
        seg_bits[:1] + woven(seg_bits[1:], traj_bits),
        seg_bits[:1] + woven(traj_bits, seg_bits[1:]),
    )


def sum_kernel(trajs, segs, loads, outs, landings, send_sems, recv_sems):
    traj, seg = lax.axis_index("traj"), lax.axis_index("seg")
    core = seg % 2
    devices = trajs * segs

    def hop(axis, stride):
        bit = ((seg if axis == "seg" else traj) // stride) % 2
        move = stride * (1 - 2 * bit)
        return bit, (move if axis == "traj" else 0 * move), (move if axis == "seg" else 0 * move)

    def steps_of(stream):
        steps = []
        for one, other in zip(*routes(trajs, segs)):
            if stream == 1:
                one, other = other, one
            bit, by_traj, by_seg = (
                (1 - core) * a + core * b for a, b in zip(hop(*one), hop(*other))
            )
            steps.append((bit, (traj + by_traj, seg + by_seg)))
        return steps

    plans = [steps_of(stream) for stream in range(len(loads))]
    count = len(plans[0])

    barrier = pltpu.get_barrier_semaphore()
    for _, partner in plans[0]:
        pl.semaphore_signal(
            barrier, inc=1, device_id=partner, device_id_type=pl.DeviceIdType.MESH
        )
    pl.semaphore_wait(barrier, count)

    lows = [0 * traj for _ in loads]
    kept = [[] for _ in loads]
    flying = [None for _ in loads]

    def send(stream, phase, source, target, partner):
        place = stream * 2 * count + phase
        flying[stream] = pltpu.make_async_remote_copy(
            src_ref=source,
            dst_ref=target,
            send_sem=send_sems.at[place],
            recv_sem=recv_sems.at[place],
            device_id=partner,
            device_id_type=pl.DeviceIdType.MESH,
        )
        flying[stream].start()

    def held(stream, phase):
        half = devices >> (phase + 1)
        bit = plans[stream][phase][0]
        if phase == 0:
            return loads[stream], bit * half, (1 - bit) * half
        begins = devices - 4 * half
        return landings[stream], begins + bit * half, begins + (1 - bit) * half

    def begin(stream, phase):
        if phase < count:
            half = devices >> (phase + 1)
            source, _, give = held(stream, phase)
            kept[stream].append(lows[stream] + plans[stream][phase][0] * half)
            lows[stream] = kept[stream][-1]
            send(
                stream,
                phase,
                source.at[pl.ds(give, half)],
                landings[stream].at[pl.ds(devices - 2 * half, half)],
                plans[stream][phase][1],
            )
        else:
            step = 2 * count - 1 - phase
            span = outs[stream].at[pl.ds(kept[stream][step], devices >> (step + 1))]
            send(stream, phase, span, span, plans[stream][step][1])

    def end(stream, phase):
        flying[stream].wait()
        if phase < count:
            half = devices >> (phase + 1)
            source, keep, _ = held(stream, phase)
            landed = devices - 2 * half
            landing = landings[stream]
            if phase == count - 1:
                outs[stream][lows[stream]] = source[keep] + landing[landed]
            else:

                @pl.loop(0, half)
                def _(i):
                    landing[landed + i] = source[keep + i] + landing[landed + i]

    for phase in range(2 * count + 1):
        for stream in range(len(loads)):
            if phase > 0:
                end(stream, phase - 1)
            if phase < 2 * count:
                begin(stream, phase)


def sum_over_devices(loads, trajs, segs):
    steps = (trajs * segs).bit_length() - 1
    number = len(loads)
    vmem = pl.BlockSpec(memory_space=pltpu.VMEM)

    def body(*refs):
        groups = [refs[i * number : (i + 1) * number] for i in range(3)]
        sum_kernel(trajs, segs, *groups, *refs[3 * number :])

    return pl.pallas_call(
        body,
        out_shape=[jax.ShapeDtypeStruct(load.shape, jnp.float32) for load in loads],
        in_specs=[vmem] * number,
        out_specs=[vmem] * number,
        scratch_shapes=[
            *(pltpu.VMEM((trajs * segs - 1, *load.shape[1:]), jnp.float32) for load in loads),
            pltpu.SemaphoreType.DMA((2 * steps * number,)),
            pltpu.SemaphoreType.DMA((2 * steps * number,)),
        ],
        compiler_params=pltpu.CompilerParams(
            collective_id=0, has_side_effects=True, vmem_limit_bytes=48 * 1024 * 1024
        ),
        cost_estimate=pl.CostEstimate(
            flops=10**9, bytes_accessed=10**7, transcendentals=0
        ),
        name="sum_over_devices",
    )(*loads)


def featurize(frames, selection):
    frame_rows, parts, atoms = frames.shape
    offset = exact_dot(jnp.swapaxes(frames, 0, 1).reshape(parts * frame_rows, atoms), selection)
    offset = offset.reshape(parts, frame_rows, -1)
    return jnp.sqrt(jnp.sum(offset * offset, axis=0) + soft_square)


def on_device(coords, pairs, lengths):
    frames = coords[0]
    frame_rows, _, atoms = frames.shape
    feature_count = pairs.shape[1]
    trajs, segs = lax.axis_size("traj"), lax.axis_size("seg")
    devices = trajs * segs
    traj, seg = lax.axis_index("traj"), lax.axis_index("seg")
    me = traj * segs + seg
    length = lengths[0]

    arriving = lax.ppermute(frames[:LAG], "seg", [(i + 1, i) for i in range(segs - 1)])
    atom = jnp.arange(atoms, dtype=jnp.int32)[:, None]
    selection = (atom == pairs[0][None]).astype(jnp.float32) - (atom == pairs[1][None]).astype(
        jnp.float32
    )
    features = featurize(frames, selection)
    lagged = jnp.concatenate([features[LAG:], featurize(arriving, selection)], axis=0)

    frame_index = seg * frame_rows + jnp.arange(frame_rows, dtype=jnp.int32)
    is_valid = (frame_index < length).astype(jnp.float32)[:, None]
    paired = (frame_index + LAG < length).astype(jnp.float32)[:, None]
    count_all = jnp.maximum(jnp.sum(is_valid), 1.0)
    count_pair = jnp.maximum(jnp.sum(paired), 1.0)
    own_all = jnp.sum(features * is_valid, axis=0) / count_all
    own_lead = jnp.sum(features * paired, axis=0) / count_pair
    own_ahead = jnp.sum(lagged * paired, axis=0) / count_pair
    centered = (features - own_all) * is_valid
    lead_rows = (features - own_lead) * paired
    ahead_rows = (lagged - own_ahead) * paired
    mine = (jnp.arange(devices) == me)[:, None]
    slot_length = jnp.where(
        (jnp.arange(trajs) == traj) & (seg == 0), length.astype(jnp.float32), 0.0
    )
    slot_length = jnp.pad(slot_length[None], ((0, 7), (0, feature_count - trajs)))

    folded_rows = (feature_count // BLOCK) * (feature_count // BLOCK + 1) // 2 * BLOCK

    def padded(slots):
        slots = jnp.concatenate(slots, axis=0).reshape(-1, BLOCK)
        loaded = folded_rows + slots.shape[0]
        share = -(-loaded // (8 * devices)) * 8
        return jnp.pad(slots, ((0, share * devices - loaded), (0, 0)))

    def unload(total):
        total = total.reshape(-1, BLOCK)
        slots = total[folded_rows:]
        per = feature_count // BLOCK
        slots = slots[: slots.shape[0] // per * per]
        return total, slots.reshape(-1, feature_count)

    loads = grams(
        centered,
        lead_rows,
        ahead_rows,
        padded([jnp.where(mine, own_all[None], 0.0), slot_length]),
        padded(
            [jnp.where(mine, own_lead[None], 0.0), jnp.where(mine, own_ahead[None], 0.0)]
        ),
    )
    loads = [load.reshape(devices, -1, BLOCK) for load in loads]
    first_total, second_total = sum_over_devices(loads, trajs, segs)

    folded_zero, slots = unload(first_total)
    all_lengths = slots[devices, :trajs]
    begins = jnp.arange(segs, dtype=jnp.float32)[None] * frame_rows
    counts = jnp.clip(all_lengths[:, None] - begins, 0.0, frame_rows).reshape(devices, 1)
    pair_counts = jnp.clip(all_lengths[:, None] - LAG - begins, 0.0, frame_rows).reshape(devices, 1)
    frames_total, pairs_total = jnp.sum(counts), jnp.sum(pair_counts)
    device_all = slots[:devices]
    mean_all = jnp.sum(device_all * counts, axis=0) / frames_total
    spread_all = device_all - mean_all
    inverse, first_factor, image = negative_inverse(
        folded_zero, spread_all * counts, spread_all, (1.0 / frames_total).reshape(1, 1)
    )

    folded_lag, slots = unload(second_total)
    device_lead, device_ahead = slots[:devices], slots[devices : 2 * devices]
    spread_lead = device_lead - jnp.sum(device_lead * pair_counts, axis=0) / pairs_total
    spread_ahead = device_ahead - jnp.sum(device_ahead * pair_counts, axis=0) / pairs_total
    shifted = (features - mean_all) * is_valid
    projected = sweeps(
        folded_lag,
        jnp.concatenate([spread_lead * pair_counts, spread_ahead * pair_counts], axis=0),
        jnp.concatenate([spread_ahead, spread_lead], axis=0),
        (0.5 / pairs_total).reshape(1, 1),
        inverse,
        first_factor,
        image,
        shifted,
    )
    return projected[None]


def solution(mesh):
    return jax.shard_map(
        on_device,
        mesh=mesh,
        in_specs=(P("traj", "seg", None, None), P(), P("traj")),
        out_specs=P("traj", "seg", None),
        check_vma=False,
    )
```
